128 devices in a mesh: space: 16 (over z_hi, y, core), filt: 8 (over z_lo, x).
Axes of the slice: x: 4, y: 4, z: 4 (z_hi: 2, z_lo: 2; z = z_hi * 2 + z_lo), core: 2. Of those that a mesh axis runs over, the one named last changes fastest.
Arguments:
- volume: bfloat16 [4, 128, 32, 1024], P(None, None, 'space'), may hold values from -6 to 6
- kernel: bfloat16 [3, 3, 3, 256, 128], P(None, None, None, 'filt'), may hold values from -0.109375 to 0.109375
- out_grad: bfloat16 [4, 256, 16, 256], P(None, 'filt', 'space'), may hold values from -6 to 6
Outputs:
- output: bfloat16 [4, 256, 16, 256], P(None, 'filt', 'space')
- input_grad: bfloat16 [4, 128, 32, 1024], P(None, None, 'space', 'filt')
- kernel_grad: float32 [3, 3, 3, 256, 128], P(None, None, None, 'filt')
The draws below stay inside these ranges and needn't reach their ends.
All inputs are finite; a program needn't handle non-finite values.
Results may differ from the reference program's by a relative error of at most 0.0034.
Values may be sent and summed in bfloat16 or wider, within the bound.
No kernel may reach another device: no remote copies, remote signals or barrier semaphores. Data moves between devices by JAX's collectives and lax.ppermute only.
A program may use at most 256 MiB of HBM per device.

```python
import jax
import jax.numpy as jnp
from jax import lax

CIN = 128
COUT = 256
EDGE = 32
SAMPLES = 4
HALF = 16


def level_of(key, extent, split, smallest, largest):
    factor_of, own = 1.0, jax.random.fold_in(key, 6)
    for position, shards_of in split:
        heights = jnp.exp(jax.random.uniform(jax.random.fold_in(own, position), (shards_of,), jnp.float32, smallest / len(split), largest / len(split)))
        factor_of = factor_of * jnp.repeat(heights, extent[position] // shards_of).reshape([-1 if axis == position else 1 for axis in range(len(extent))])
    return factor_of


def scatter_about(stream_key, extent, scale, most, split=(), held_as=jnp.bfloat16):
    gain = level_of(stream_key, extent, split, -0.22, 0.18) if split else 1.0
    entries = jax.random.normal(stream_key, extent, jnp.float32) * scale * gain
    return jnp.minimum(jnp.maximum(entries, -most), most).astype(held_as)


def setup_inputs(seed: int = 0) -> dict:
    streams_of = jax.random.split(jax.random.key(seed), 4)
    volume = scatter_about(streams_of[0], (SAMPLES, CIN, EDGE, EDGE * EDGE), 1.0, 6.0, ((2, 16),))
    kernel = scatter_about(streams_of[1], (3, 3, 3, COUT, CIN), (27 * CIN) ** -0.5, 0.109375, ((3, 8),))
    out_grad = scatter_about(streams_of[2], (SAMPLES, COUT, HALF, HALF * HALF), 1.0, 6.0, ((1, 8), (2, 16)))
    return dict(volume=volume, kernel=kernel, out_grad=out_grad)


def convolve(volume_in, weights):
    return lax.conv_general_dilated(volume_in, weights, (2, 2, 2), ((1, 0), (1, 0), (1, 0)), dimension_numbers=('NCDHW', 'DHWOI', 'NCDHW'), precision=lax.Precision.HIGHEST, preferred_element_type=jnp.float32)

def reference(volume, kernel, out_grad):
    vol_wide = volume.astype(jnp.float32).reshape(SAMPLES, CIN, EDGE, EDGE, EDGE)
    ker_wide = kernel.astype(jnp.float32)
    grad_wide = out_grad.astype(jnp.float32).reshape(SAMPLES, COUT, HALF, HALF, HALF)
    output = convolve(vol_wide, ker_wide).astype(jnp.bfloat16).reshape(SAMPLES, COUT, HALF, HALF * HALF)
    unused, puller = jax.vjp(convolve, vol_wide, ker_wide)
    vol_term, kernel_grad = puller(grad_wide)
    input_grad = vol_term.astype(jnp.bfloat16).reshape(SAMPLES, CIN, EDGE, EDGE * EDGE)
    return (output, input_grad, kernel_grad)
```

```python
import jax
import jax.numpy as jnp
from jax import lax
from jax.experimental import pallas as pl
from jax.experimental.pallas import tpu as pltpu
from jax.sharding import PartitionSpec as P

B = 4
CIN = 128
EDGE = 32
HALF = 16
F32 = jnp.float32
BF16 = jnp.bfloat16
NT = (((1,), (1,)), ((), ()))
ROWS = 896


def iota(shape, axis):
    return lax.broadcasted_iota(jnp.int32, shape, axis)


def conv_kernel(vol_ref, ker_ref, g_ref, gn_ref, own_ref, send_ref, dw_ref,
                perm, select, planes, cols):
    step = pl.program_id(0)

    @pl.when(step == 0)
    def _():
        row, col = iota((256, 256), 0), iota((256, 256), 1)
        source = (row & 15) * 16 + ((row >> 4) & 7) * 2 + (row >> 7)
        perm[...] = jnp.where(col == source, 1.0, 0.0).astype(BF16)
        row, col = iota((192, 128), 0), iota((192, 128), 1)
        depth = (row & 15) * 2 + (row >> 6) - 1
        wanted = (col == ((row >> 4) & 3) * 32 + depth) & (depth >= 0)
        select[...] = jnp.where(wanted, 1.0, 0.0).astype(BF16)
        dw_ref[...] = jnp.zeros_like(dw_ref)
        for x in range(2):
            for k in range(3):
                planes[x, k, 0] = jnp.zeros((HALF, CIN), BF16)

    for group in range(8):
        block = vol_ref[0, group * 256:(group + 1) * 256, :]
        moved = jnp.dot(perm[...], block, preferred_element_type=F32).astype(BF16)
        for x in range(2):
            for lt in range(8):
                start = (x * 8 + lt) * 16
                cols[lt, x * 128 + group * 16:x * 128 + group * 16 + 16, :] = moved[start:start + 16]
    for lt in range(8):
        turned = lax.dot_general(select[...], cols[lt], NT, preferred_element_type=F32).astype(BF16)
        for k in range(3):
            for y in range(4):
                start = k * 64 + y * 16
                for x in range(2):
                    planes[x, k, 1 + 4 * lt + y] = turned[start:start + 16, x * 128:(x + 1) * 128]

    def columns(x):
        parts = []
        for j in range(3):
            for k in range(3):
                rows = [planes[x, k, 2 * q + j] for q in range(HALF)]
                parts.append(jnp.concatenate(rows, 0))
        return jnp.concatenate(parts, 1)

    def weights(i):
        return jnp.concatenate([ker_ref[i * 9 + t] for t in range(9)], 1)

    grad = g_ref[0]
    pair = jnp.concatenate([grad, gn_ref[0]], 0)
    even = columns(0)
    here = lax.dot_general(weights(1), even, NT, preferred_element_type=F32)
    back_even = jnp.dot(grad, even, preferred_element_type=F32)
    odd = columns(1)
    both = lax.dot_general(
        jnp.concatenate([weights(2), weights(0)], 0), odd, NT, preferred_element_type=F32
    )
    back_odd = jnp.dot(pair, odd, preferred_element_type=F32)
    own_ref[0] = here + both[:32]
    send_ref[0] = both[32:]
    for t in range(9):
        lanes = slice(t * 128, (t + 1) * 128)
        dw_ref[t * 32:(t + 1) * 32] += back_odd[32:, lanes]
        dw_ref[(9 + t) * 32:(10 + t) * 32] += back_even[:, lanes]
        dw_ref[(18 + t) * 32:(19 + t) * 32] += back_odd[:32, lanes]


def conv_local(vol, ker, g, gn):
    per_sample = lambda *shape: pl.BlockSpec((1,) + shape, lambda b: (b,) + (0,) * len(shape))
    whole = lambda *shape: pl.BlockSpec(shape, lambda b: (0,) * len(shape))
    return pl.pallas_call(
        conv_kernel,
        grid=(B,),
        in_specs=[per_sample(2048, 128), whole(27, 32, CIN), per_sample(32, 256), per_sample(32, 256)],
        out_specs=[per_sample(32, 256), per_sample(32, 256), whole(ROWS, CIN)],
        out_shape=[
            jax.ShapeDtypeStruct((B, 32, 256), F32),
            jax.ShapeDtypeStruct((B, 32, 256), F32),
            jax.ShapeDtypeStruct((ROWS, CIN), F32),
        ],
        scratch_shapes=[
            pltpu.VMEM((256, 256), BF16),
            pltpu.VMEM((192, 128), BF16),
            pltpu.VMEM((2, 3, EDGE + 1, HALF, CIN), BF16),
            pltpu.VMEM((8, 256, 128), BF16),
        ],
        compiler_params=pltpu.CompilerParams(vmem_limit_bytes=40 * 1024 * 1024),
        cost_estimate=pl.CostEstimate(flops=6_000_000_000, bytes_accessed=4_000_000, transcendentals=0),
        name="conv_local",
    )(vol, ker, g, gn)


def spread_kernel(g_ref, gn_ref, out_ref):
    for b in range(B):
        for f in range(8):
            parts = []
            for ref in (g_ref, gn_ref):
                whole = jnp.concatenate([ref[b], jnp.zeros((32, 128), BF16)], 1)
                parts.append(whole[:, 32 * f:32 * f + 64])
            out_ref[f, b] = jnp.concatenate(parts, 1)


def spread(g, gn):
    return pl.pallas_call(
        spread_kernel,
        out_shape=jax.ShapeDtypeStruct((8, B, 32, 128), BF16),
        name="spread",
    )(g, gn)


def input_grad_kernel(ker_ref, g_ref, out_ref, grads, mixed, paired):
    last = (iota((128, 256), 0) & 15) == 15
    for b in range(B):
        block = g_ref[:, b].reshape(256, 128).astype(F32)
        turned = jnp.transpose(block)
        later = jnp.where(last, 0.0, pltpu.roll(turned, 127, 0))
        for shift, value in enumerate((turned, later)):
            low = value.astype(BF16)
            for p in range(2):
                for q in range(3):
                    start = p * 64 + q * 16
                    grads[p, shift, q, b] = low[start:start + 16]

    def lhs(p, qs, rs):
        rows = [grads[p, rs, qs + q, b] for q in range(2) for b in range(B)]
        return jnp.concatenate(rows, 0)

    def tap(i, j, k):
        return ker_ref[:, i * 9 + j * 3 + k].reshape(256, CIN)

    choices = (((1, 0),), ((2, 0), (0, 1)))
    for py in range(2):
        for pz in range(2):
            total = jnp.zeros((128, 256), F32)
            extra = jnp.zeros((128, 128), F32)
            for j, qs in choices[py]:
                for k, rs in choices[pz]:
                    two = jnp.concatenate([tap(1, j, k), tap(2, j, k)], 1)
                    total += jnp.dot(lhs(0, qs, rs), two, preferred_element_type=F32)
                    extra += jnp.dot(lhs(1, qs, rs), tap(0, j, k), preferred_element_type=F32)
            values = (total[:, :128], total[:, 128:] + extra)
            for px in range(2):
                for q in range(2):
                    for b in range(B):
                        start = (q * B + b) * 16
                        mixed[px, b, pl.ds((2 * q + py) * 32 + pz, 16, stride=2), :] = (
                            values[px][start:start + 16]
                        )
    for b in range(B):
        for px in range(2):
            paired[b, pl.ds(px, CIN, stride=2), :] = jnp.transpose(mixed[px, b])
        out_ref[b] = paired[b].astype(BF16)


def input_grad_local(ker_all, g_all):
    return pl.pallas_call(
        input_grad_kernel,
        out_shape=jax.ShapeDtypeStruct((B, 2 * CIN, 128), BF16),
        scratch_shapes=[
            pltpu.VMEM((2, 2, 3, B, HALF, 256), BF16),
            pltpu.VMEM((2, B, 128, CIN), F32),
            pltpu.VMEM((B, 2 * CIN, 128), F32),
        ],
        compiler_params=pltpu.CompilerParams(vmem_limit_bytes=40 * 1024 * 1024),
        cost_estimate=pl.CostEstimate(flops=2_000_000_000, bytes_accessed=3_000_000, transcendentals=0),
        name="input_grad_local",
    )(ker_all, g_all)


def sum_kernel(parts_ref, out_ref):
    total = parts_ref[0]
    for i in range(1, 16):
        total = total + parts_ref[i]
    for i in range(16):
        out_ref[i] = total


def sum_and_copy(parts):
    return pl.pallas_call(
        sum_kernel,
        out_shape=jax.ShapeDtypeStruct(parts.shape, parts.dtype),
        name="sum_and_copy",
    )(parts)


def swap(values, axis):
    return lax.all_to_all(values, axis, split_axis=0, concat_axis=0, tiled=True)


def body(volume, kernel, out_grad):
    spaces = lax.axis_size("space")
    g = out_grad.reshape(B, 32, 256)
    ker = kernel.reshape(27, 32, CIN)
    g_next = lax.ppermute(g, "space", [(i + 1, i) for i in range(spaces - 1)])
    ker_all = swap(jnp.broadcast_to(ker[None], (8, 27, 32, CIN)), "filt")
    g_all = swap(spread(g, g_next), "filt")
    vol = volume.reshape(B, CIN, 2, 8, 128).transpose(0, 1, 3, 2, 4).reshape(B, 2048, 128)
    own, send, dw = conv_local(vol, ker, g, g_next)
    came = lax.ppermute(send, "space", [(i, i + 1) for i in range(spaces - 1)])
    dw_mine = sum_and_copy(swap(dw.reshape(16, 56, CIN), "space"))
    dw_all = swap(dw_mine, "space").reshape(ROWS, CIN)
    output = (own + came).astype(BF16).reshape(B, 32, 1, 256)
    input_grad = input_grad_local(ker_all, g_all).reshape(B, CIN, 2, 128)
    kernel_grad = dw_all[:864].reshape(3, 3, 3, 32, CIN)
    return (output, input_grad, kernel_grad)


def solution(mesh):
    return jax.shard_map(
        body,
        mesh=mesh,
        in_specs=(
            P(None, None, "space", None),
            P(None, None, None, "filt", None),
            P(None, "filt", "space", None),
        ),
        out_specs=(
            P(None, "filt", "space", None),
            P(None, None, "space", "filt"),
            P(None, None, None, "filt", None),
        ),
        check_vma=False,
    )
```

```python
import jax
import jax.numpy as jnp
from jax import lax
from jax.experimental import pallas as pl
from jax.experimental.pallas import tpu as pltpu
from jax.sharding import PartitionSpec as P

B = 4
CIN = 128
EDGE = 32
HALF = 16
F32 = jnp.float32
BF16 = jnp.bfloat16
NT = (((1,), (1,)), ((), ()))
TAPS = 14
PACKED = TAPS * 32 + 64
ROWS = 896


def iota(shape, axis):
    return lax.broadcasted_iota(jnp.int32, shape, axis)


def conv_kernel(vol_ref, ker_ref, g_ref, gn_ref, own_ref, send_ref, dw_ref,
                perm, select, planes, cols):
    step = pl.program_id(0)

    @pl.when(step == 0)
    def _():
        row, col = iota((256, 256), 0), iota((256, 256), 1)
        source = (row & 15) * 16 + ((row >> 4) & 7) * 2 + (row >> 7)
        perm[...] = jnp.where(col == source, 1.0, 0.0).astype(BF16)
        row, col = iota((192, 128), 0), iota((192, 128), 1)
        depth = (row & 15) * 2 + (row >> 6) - 1
        wanted = (col == ((row >> 4) & 3) * 32 + depth) & (depth >= 0)
        select[...] = jnp.where(wanted, 1.0, 0.0).astype(BF16)
        dw_ref[...] = jnp.zeros_like(dw_ref)
        for x in range(2):
            for k in range(3):
                planes[x, k, 0] = jnp.zeros((HALF, CIN), BF16)

    for group in range(8):
        block = vol_ref[0, group * 256:(group + 1) * 256, :]
        moved = jnp.dot(perm[...], block, preferred_element_type=F32).astype(BF16)
        for x in range(2):
            for lt in range(8):
                start = (x * 8 + lt) * 16
                cols[lt, x * 128 + group * 16:x * 128 + group * 16 + 16, :] = moved[start:start + 16]
    for lt in range(8):
        turned = lax.dot_general(select[...], cols[lt], NT, preferred_element_type=F32).astype(BF16)
        for k in range(3):
            for y in range(4):
                start = k * 64 + y * 16
                for x in range(2):
                    planes[x, k, 1 + 4 * lt + y] = turned[start:start + 16, x * 128:(x + 1) * 128]

    def columns(x):
        parts = []
        for j in range(3):
            for k in range(3):
                rows = [planes[x, k, 2 * q + j] for q in range(HALF)]
                parts.append(jnp.concatenate(rows, 0))
        return jnp.concatenate(parts, 1)

    def weights(i):
        return jnp.concatenate([ker_ref[i * 9 + t] for t in range(9)], 1)

    grad = g_ref[0]
    pair = jnp.concatenate([grad, gn_ref[0]], 0)
    even = columns(0)
    here = lax.dot_general(weights(1), even, NT, preferred_element_type=F32)
    back_even = jnp.dot(grad, even, preferred_element_type=F32)
    odd = columns(1)
    both = lax.dot_general(
        jnp.concatenate([weights(2), weights(0)], 0), odd, NT, preferred_element_type=F32
    )
    back_odd = jnp.dot(pair, odd, preferred_element_type=F32)
    own_ref[0] = here + both[:32]
    send_ref[0] = both[32:]
    for t in range(9):
        lanes = slice(t * 128, (t + 1) * 128)
        dw_ref[t * 32:(t + 1) * 32] += back_odd[32:, lanes]
        dw_ref[(9 + t) * 32:(10 + t) * 32] += back_even[:, lanes]
        dw_ref[(18 + t) * 32:(19 + t) * 32] += back_odd[:32, lanes]


def conv_local(vol, ker, g, gn):
    per_sample = lambda *shape: pl.BlockSpec((1,) + shape, lambda b: (b,) + (0,) * len(shape))
    whole = lambda *shape: pl.BlockSpec(shape, lambda b: (0,) * len(shape))
    return pl.pallas_call(
        conv_kernel,
        grid=(B,),
        in_specs=[per_sample(2048, 128), whole(27, 32, CIN), per_sample(32, 256), per_sample(32, 256)],
        out_specs=[per_sample(32, 256), per_sample(32, 256), whole(ROWS, CIN)],
        out_shape=[
            jax.ShapeDtypeStruct((B, 32, 256), F32),
            jax.ShapeDtypeStruct((B, 32, 256), F32),
            jax.ShapeDtypeStruct((ROWS, CIN), F32),
        ],
        scratch_shapes=[
            pltpu.VMEM((256, 256), BF16),
            pltpu.VMEM((192, 128), BF16),
            pltpu.VMEM((2, 3, EDGE + 1, HALF, CIN), BF16),
            pltpu.VMEM((8, 256, 128), BF16),
        ],
        compiler_params=pltpu.CompilerParams(vmem_limit_bytes=40 * 1024 * 1024),
        cost_estimate=pl.CostEstimate(flops=6_000_000_000, bytes_accessed=4_000_000, transcendentals=0),
        name="conv_local",
    )(vol, ker, g, gn)


def pack_kernel(ker_ref, g_ref, out_ref):
    core = lax.rem(lax.axis_index("space"), 2)
    half = ker_ref[pl.ds(core * 13, TAPS)].reshape(TAPS * 32, CIN)
    for f in range(8):
        out_ref[f, :TAPS * 32] = half
    for b in range(B):
        whole = jnp.concatenate([g_ref[b], jnp.zeros((32, 128), BF16)], 1)
        start, lane = TAPS * 32 + (b // 2) * 32, (b % 2) * 64
        for f in range(8):
            out_ref[f, start:start + 32, lane:lane + 64] = whole[:, 32 * f:32 * f + 64]


def pack(ker, g):
    return pl.pallas_call(
        pack_kernel,
        out_shape=jax.ShapeDtypeStruct((8, PACKED, 128), BF16),
        name="pack",
    )(ker, g)


def input_grad_kernel(mine_ref, other_ref, next_ref, out_ref, halves, grads, mixed, paired):
    core = lax.rem(lax.axis_index("space"), 2)
    halves[core] = mine_ref[:, :TAPS * 32]
    halves[1 - core] = other_ref[:, :TAPS * 32]
    last = (iota((128, 256), 0) & 15) == 15
    for p, (ref, first) in enumerate(((mine_ref, TAPS * 32), (next_ref, 0))):
        for two in range(B // 2):
            start = first + two * 32
            block = ref[:, start:start + 32].reshape(256, 128).astype(F32)
            turned = jnp.transpose(block)
            later = jnp.where(last, 0.0, pltpu.roll(turned, 127, 0))
            for shift, value in enumerate((turned, later)):
                low = value.astype(BF16)
                for b in range(2):
                    for q in range(3):
                        start = b * 64 + q * 16
                        grads[p, shift, q, 2 * two + b] = low[start:start + 16]

    def lhs(p, qs, rs):
        rows = [grads[p, rs, qs + q, b] for q in range(2) for b in range(B)]
        return jnp.concatenate(rows, 0)

    def tap(i, j, k):
        t = i * 9 + j * 3 + k
        half, place = (0, t) if t < TAPS else (1, t - 13)
        return halves[half, :, place * 32:place * 32 + 32].reshape(256, CIN)

    choices = (((1, 0),), ((2, 0), (0, 1)))
    for py in range(2):
        for pz in range(2):
            total = jnp.zeros((128, 256), F32)
            extra = jnp.zeros((128, 128), F32)
            for j, qs in choices[py]:
                for k, rs in choices[pz]:
                    two = jnp.concatenate([tap(1, j, k), tap(2, j, k)], 1)
                    total += jnp.dot(lhs(0, qs, rs), two, preferred_element_type=F32)
                    extra += jnp.dot(lhs(1, qs, rs), tap(0, j, k), preferred_element_type=F32)
            values = (total[:, :128], total[:, 128:] + extra)
            for px in range(2):
                for q in range(2):
                    for b in range(B):
                        start = (q * B + b) * 16
                        mixed[px, b, pl.ds((2 * q + py) * 32 + pz, 16, stride=2), :] = (
                            values[px][start:start + 16]
                        )
    for b in range(B):
        for px in range(2):
            paired[b, pl.ds(px, CIN, stride=2), :] = jnp.transpose(mixed[px, b])
        out_ref[b] = paired[b].astype(BF16)


def input_grad_local(mine, other, following):
    return pl.pallas_call(
        input_grad_kernel,
        out_shape=jax.ShapeDtypeStruct((B, 2 * CIN, 128), BF16),
        scratch_shapes=[
            pltpu.VMEM((2, 8, TAPS * 32, CIN), BF16),
            pltpu.VMEM((2, 2, 3, B, HALF, 256), BF16),
            pltpu.VMEM((2, B, 128, CIN), F32),
            pltpu.VMEM((B, 2 * CIN, 128), F32),
        ],
        compiler_params=pltpu.CompilerParams(vmem_limit_bytes=40 * 1024 * 1024),
        cost_estimate=pl.CostEstimate(flops=2_000_000_000, bytes_accessed=3_000_000, transcendentals=0),
        name="input_grad_local",
    )(mine, other, following)


def sum_kernel(parts_ref, out_ref):
    total = parts_ref[0]
    for i in range(1, 16):
        total = total + parts_ref[i]
    for i in range(16):
        out_ref[i] = total.astype(BF16)


def sum_and_copy(parts):
    return pl.pallas_call(
        sum_kernel,
        out_shape=jax.ShapeDtypeStruct(parts.shape, BF16),
        name="sum_and_copy",
    )(parts)


def swap(values, axis):
    return lax.all_to_all(values, axis, split_axis=0, concat_axis=0, tiled=True)


def body(volume, kernel, out_grad):
    spaces = lax.axis_size("space")
    g = out_grad.reshape(B, 32, 256)
    ker = kernel.reshape(27, 32, CIN)
    to_previous = [(i + 1, i) for i in range(spaces - 1)]
    to_next = [(i, i + 1) for i in range(spaces - 1)]
    to_other_core = [(i, i ^ 1) for i in range(spaces)]
    g_next = lax.ppermute(g, "space", to_previous)
    mine = swap(pack(ker, g), "filt")
    vol = volume.reshape(B, CIN, 2, 8, 128).transpose(0, 1, 3, 2, 4).reshape(B, 2048, 128)
    own, send, dw = conv_local(vol, ker, g, g_next)
    dw, mine = lax.optimization_barrier((dw, mine))
    came = lax.ppermute(send, "space", to_next)
    other = lax.ppermute(mine, "space", to_other_core)
    following = lax.ppermute(mine[:, TAPS * 32:], "space", to_previous)
    dw_mine = sum_and_copy(swap(dw.reshape(16, 56, CIN), "space"))
    dw_all = swap(dw_mine, "space").reshape(ROWS, CIN)
    output = (own + came).astype(BF16).reshape(B, 32, 1, 256)
    input_grad = input_grad_local(mine, other, following).reshape(B, CIN, 2, 128)
    kernel_grad = dw_all[:864].astype(F32).reshape(3, 3, 3, 32, CIN)
    return (output, input_grad, kernel_grad)


def solution(mesh):
    return jax.shard_map(
        body,
        mesh=mesh,
        in_specs=(
            P(None, None, "space", None),
            P(None, None, None, "filt", None),
            P(None, "filt", "space", None),
        ),
        out_specs=(
            P(None, "filt", "space", None),
            P(None, None, "space", "filt"),
            P(None, None, None, "filt", None),
        ),
        check_vma=False,
    )
```

```python
import jax
import jax.numpy as jnp
from jax import lax
from jax.experimental import pallas as pl
from jax.experimental.pallas import tpu as pltpu
from jax.sharding import PartitionSpec as P

B = 4
CIN = 128
EDGE = 32
HALF = 16
F32 = jnp.float32
BF16 = jnp.bfloat16
NT = (((1,), (1,)), ((), ()))
FULL = 63_000_000
TAPS = 14
PACKED = TAPS + 2
ROWS = 896
OWN = 56


def iota(shape, axis):
    return lax.broadcasted_iota(jnp.int32, shape, axis)


def columns(plane):
    parts = []
    for j in range(3):
        for k in range(3):
            parts.append(jnp.concatenate([plane(k, 2 * q + j) for q in range(HALF)], 0))
    return jnp.concatenate(parts, 1)


def conv_kernel(vol_ref, ker_ref, g_ref, own_ref, send_ref, dw_ref, odd_ref,
                total, raw, arrived, ker_in, grads_in, perm, select, planes, cols):
    step = pl.program_id(0)

    def fetch(b):
        return pltpu.make_async_copy(vol_ref.at[b], raw.at[b], arrived.at[b])

    others = [
        pltpu.make_async_copy(ker_ref, ker_in, arrived.at[B]),
        pltpu.make_async_copy(g_ref, grads_in, arrived.at[B + 1]),
    ]

    @pl.when(step == 0)
    def _():
        fetch(0).start()
        for copy in others:
            copy.start()
        for b in range(1, B):
            fetch(b).start()

    @pl.when(step == 0)
    def _():
        row, col = iota((256, 256), 0), iota((256, 256), 1)
        source = (row & 15) * 16 + ((row >> 4) & 7) * 2 + (row >> 7)
        perm[...] = jnp.where(col == source, 1.0, 0.0).astype(BF16)
        row, col = iota((192, 128), 0), iota((192, 128), 1)
        depth = (row & 15) * 2 + (row >> 6) - 1
        wanted = (col == ((row >> 4) & 3) * 32 + depth) & (depth >= 0)
        select[...] = jnp.where(wanted, 1.0, 0.0).astype(BF16)
        total[...] = jnp.zeros_like(total)
        dw_ref[...] = jnp.zeros_like(dw_ref)
        for k in range(3):
            planes[k, 0] = jnp.zeros((HALF, CIN), BF16)

    fetch(step).wait()
    wide = jnp.concatenate([raw[step, g * 256:(g + 1) * 256] for g in range(8)], 1)
    moved = jnp.dot(perm[...], wide, preferred_element_type=F32).astype(BF16)
    for lt in range(8):
        for x in range(2):
            start = (x * 8 + lt) * 16
            for g in range(8):
                cols[lt, x * 128 + g * 16:x * 128 + g * 16 + 16, :] = (
                    moved[start:start + 16, g * 128:(g + 1) * 128]
                )
    for k in range(3):
        odd_ref[0, k, 0] = jnp.zeros((HALF, CIN), BF16)
    for lt in range(8):
        turned = lax.dot_general(select[...], cols[lt], NT, preferred_element_type=F32).astype(BF16)
        for k in range(3):
            for y in range(4):
                start = k * 64 + y * 16
                planes[k, 1 + 4 * lt + y] = turned[start:start + 16, :128]
                odd_ref[0, k, 1 + 4 * lt + y] = turned[start:start + 16, 128:]

    @pl.when(step == 0)
    def _():
        for copy in others:
            copy.wait()

    def weights(i):
        return jnp.concatenate([ker_in[i * 9 + t] for t in range(9)], 1)

    grad = grads_in[step]
    even = columns(lambda k, y: planes[k, y])
    here = lax.dot_general(weights(1), even, NT, preferred_element_type=F32)
    back_even = jnp.dot(grad, even, preferred_element_type=F32)
    odd = columns(lambda k, y: odd_ref[0, k, y])
    both = lax.dot_general(
        jnp.concatenate([weights(2), weights(0)], 0), odd, NT, preferred_element_type=F32
    )
    back_odd = jnp.dot(grad, odd, preferred_element_type=F32)
    own_ref[0] = here + both[:32]
    send_ref[0] = both[32:]
    for t in range(9):
        lanes = slice(t * 128, (t + 1) * 128)
        total[t * 32:(t + 1) * 32] += back_even[:, lanes]
        total[(9 + t) * 32:(10 + t) * 32] += back_odd[:, lanes]

    @pl.when(step == B - 1)
    def _():
        dw_ref[288:864] = total[...].astype(BF16)


def conv_local(vol, ker, g):
    per_sample = lambda *shape: pl.BlockSpec((1,) + shape, lambda b: (b,) + (0,) * len(shape))
    whole = lambda *shape: pl.BlockSpec(shape, lambda b: (0,) * len(shape))
    return pl.pallas_call(
        conv_kernel,
        grid=(B,),
        in_specs=[pl.BlockSpec(memory_space=pltpu.HBM)] * 3,
        out_specs=[per_sample(32, 256), per_sample(32, 256), whole(ROWS, CIN), per_sample(3, EDGE + 1, HALF, CIN)],
        out_shape=[
            jax.ShapeDtypeStruct((B, 32, 256), F32),
            jax.ShapeDtypeStruct((B, 32, 256), F32),
            jax.ShapeDtypeStruct((ROWS, CIN), BF16),
            jax.ShapeDtypeStruct((B, 3, EDGE + 1, HALF, CIN), BF16),
        ],
        scratch_shapes=[
            pltpu.VMEM((576, CIN), F32),
            pltpu.VMEM((B, 2048, 128), BF16),
            pltpu.SemaphoreType.DMA((B + 2,)),
            pltpu.VMEM((27, 32, CIN), BF16),
            pltpu.VMEM((B, 32, 256), BF16),
            pltpu.VMEM((256, 256), BF16),
            pltpu.VMEM((192, 128), BF16),
            pltpu.VMEM((3, EDGE + 1, HALF, CIN), BF16),
            pltpu.VMEM((8, 256, 128), BF16),
        ],
        compiler_params=pltpu.CompilerParams(vmem_limit_bytes=FULL),
        cost_estimate=pl.CostEstimate(flops=6_000_000_000, bytes_accessed=4_000_000, transcendentals=0),
        name="conv_local",
    )(vol, ker, g)


def next_kernel(odd_ref, gn_ref, _, dw_ref, odd, grad, low, arrived):
    copies = [pltpu.make_async_copy(gn_ref, grad, arrived.at[B])]
    for b in range(B):
        copies.append(pltpu.make_async_copy(odd_ref.at[b], odd.at[b], arrived.at[b]))
    for copy in copies:
        copy.start()
    copies[0].wait()
    total = None
    for b in range(B):
        copies[1 + b].wait()
        back = jnp.dot(
            grad[b], columns(lambda k, y: odd[b, k, y]), preferred_element_type=F32
        )
        total = back if total is None else total + back
    for t in range(9):
        low[t * 32:(t + 1) * 32] = total[:, t * 128:(t + 1) * 128].astype(BF16)
    last = pltpu.make_async_copy(low, dw_ref.at[pl.ds(0, 288)], arrived.at[B + 1])
    last.start()
    last.wait()


def next_local(odd, gn, dw):
    return pl.pallas_call(
        next_kernel,
        in_specs=[pl.BlockSpec(memory_space=pltpu.HBM)] * 3,
        out_specs=pl.BlockSpec(memory_space=pltpu.HBM),
        out_shape=jax.ShapeDtypeStruct((ROWS, CIN), BF16),
        scratch_shapes=[
            pltpu.VMEM((B, 3, EDGE + 1, HALF, CIN), BF16),
            pltpu.VMEM((B, 32, 256), BF16),
            pltpu.VMEM((288, CIN), BF16),
            pltpu.SemaphoreType.DMA((B + 2,)),
        ],
        input_output_aliases={2: 0},
        compiler_params=pltpu.CompilerParams(vmem_limit_bytes=FULL),
        cost_estimate=pl.CostEstimate(flops=1_000_000_000, bytes_accessed=2_000_000, transcendentals=0),
        name="next_local",
    )(odd, gn, dw)


def pack_kernel(ker_ref, g_ref, out_ref, half, grad, cells, sent):
    core = lax.rem(lax.axis_index("space"), 2)
    fetch_half = pltpu.make_async_copy(ker_ref.at[pl.ds(core * 13, TAPS)], half, sent.at[8])
    fetch_grad = pltpu.make_async_copy(g_ref, grad, sent.at[9])
    fetch_half.start()
    fetch_grad.start()
    fetch_half.wait()
    copies = [
        pltpu.make_async_copy(half, out_ref.at[f, pl.ds(0, TAPS)], sent.at[f])
        for f in range(8)
    ]
    for copy in copies:
        copy.start()
    fetch_grad.wait()
    for b in range(B):
        whole = jnp.concatenate([grad[b], jnp.zeros((32, 128), BF16)], 1)
        lane = (b % 2) * 64
        for f in range(8):
            cells[f, b // 2, :, lane:lane + 64] = whole[:, 32 * f:32 * f + 64]
    last = pltpu.make_async_copy(cells, out_ref.at[:, pl.ds(TAPS, 2)], sent.at[10])
    last.start()
    for copy in copies:
        copy.wait()
    last.wait()


def pack(ker, g):
    return pl.pallas_call(
        pack_kernel,
        in_specs=[pl.BlockSpec(memory_space=pltpu.HBM)] * 2,
        out_specs=pl.BlockSpec(memory_space=pltpu.HBM),
        out_shape=jax.ShapeDtypeStruct((8, PACKED, 32, 128), BF16),
        scratch_shapes=[
            pltpu.VMEM((TAPS, 32, CIN), BF16),
            pltpu.VMEM((B, 32, 256), BF16),
            pltpu.VMEM((8, 2, 32, 128), BF16),
            pltpu.SemaphoreType.DMA((11,)),
        ],
        compiler_params=pltpu.CompilerParams(vmem_limit_bytes=FULL),
        name="pack",
    )(ker, g)


def input_grad_kernel(mine_ref, other_ref, next_ref, out_ref, halves, grads, mixed, paired):
    core = lax.rem(lax.axis_index("space"), 2)
    halves[core] = mine_ref[:, :TAPS]
    halves[1 - core] = other_ref[:, :TAPS]
    last = (iota((128, 256), 0) & 15) == 15
    for p, (ref, first) in enumerate(((mine_ref, TAPS), (next_ref, 0))):
        for two in range(B // 2):
            block = ref[:, first + two].reshape(256, 128).astype(F32)
            turned = jnp.transpose(block)
            later = jnp.where(last, 0.0, pltpu.roll(turned, 127, 0))
            for shift, value in enumerate((turned, later)):
                low = value.astype(BF16)
                for b in range(2):
                    for q in range(3):
                        start = b * 64 + q * 16
                        grads[p, shift, q, 2 * two + b] = low[start:start + 16]

    def lhs(p, qs, rs):
        rows = [grads[p, rs, qs + q, b] for q in range(2) for b in range(B)]
        return jnp.concatenate(rows, 0)

    def tap(i, j, k):
        t = i * 9 + j * 3 + k
        half, place = (0, t) if t < TAPS else (1, t - 13)
        return halves[half, :, place].reshape(256, CIN)

    choices = (((1, 0),), ((2, 0), (0, 1)))
    for py in range(2):
        for pz in range(2):
            total = jnp.zeros((128, 256), F32)
            extra = jnp.zeros((128, 128), F32)
            for j, qs in choices[py]:
                for k, rs in choices[pz]:
                    two = jnp.concatenate([tap(1, j, k), tap(2, j, k)], 1)
                    total += jnp.dot(lhs(0, qs, rs), two, preferred_element_type=F32)
                    extra += jnp.dot(lhs(1, qs, rs), tap(0, j, k), preferred_element_type=F32)
            values = (total[:, :128], total[:, 128:] + extra)
            for px in range(2):
                for q in range(2):
                    for b in range(B):
                        start = (q * B + b) * 16
                        mixed[px, b, pl.ds((2 * q + py) * 32 + pz, 16, stride=2), :] = (
                            values[px][start:start + 16]
                        )
    for b in range(B):
        for px in range(2):
            paired[b, pl.ds(px, CIN, stride=2), :] = jnp.transpose(mixed[px, b])
        out_ref[b] = paired[b].astype(BF16)


def input_grad_local(mine, other, following):
    return pl.pallas_call(
        input_grad_kernel,
        out_shape=jax.ShapeDtypeStruct((B, 2 * CIN, 128), BF16),
        scratch_shapes=[
            pltpu.VMEM((2, 8, TAPS, 32, CIN), BF16),
            pltpu.VMEM((2, 2, 3, B, HALF, 256), BF16),
            pltpu.VMEM((2, B, 128, CIN), F32),
            pltpu.VMEM((B, 2 * CIN, 128), F32),
        ],
        compiler_params=pltpu.CompilerParams(vmem_limit_bytes=24 * 1024 * 1024),
        cost_estimate=pl.CostEstimate(flops=2_000_000_000, bytes_accessed=3_000_000, transcendentals=0),
        name="input_grad_local",
    )(mine, other, following)


SMALL = pltpu.CompilerParams(vmem_limit_bytes=4 * 1024 * 1024)


def sum_kernel(parts_ref, out_ref):
    total = parts_ref[0].astype(F32)
    for i in range(1, 16):
        total = total + parts_ref[i].astype(F32)
    for i in range(16):
        out_ref[i] = total.astype(BF16)


def sum_and_copy(parts):
    return pl.pallas_call(
        sum_kernel,
        out_shape=jax.ShapeDtypeStruct(parts.shape, BF16),
        compiler_params=SMALL,
        name="sum_and_copy",
    )(parts)


def swap(values, axis):
    return lax.all_to_all(values, axis, split_axis=0, concat_axis=0, tiled=True)


def body(volume, kernel, out_grad):
    spaces = lax.axis_size("space")
    g = out_grad.reshape(B, 32, 256)
    ker = kernel.reshape(27, 32, CIN)
    to_previous = [(i + 1, i) for i in range(spaces - 1)]
    to_next = [(i, i + 1) for i in range(spaces - 1)]
    g_next = lax.ppermute(g, "space", to_previous)
    packed = pack(ker, g)
    vol = volume.reshape(B, CIN, 2, 8, 128).transpose(0, 1, 3, 2, 4).reshape(B, 2048, 128)
    mine = swap(packed, "filt")
    own, send, dw, odd = conv_local(vol, ker, g)
    dw = next_local(odd, g_next, dw)
    dw, mine = lax.optimization_barrier((dw, mine))
    came = lax.ppermute(send, "space", to_next)
    other = lax.ppermute(mine, "space", [(i, i ^ 1) for i in range(spaces)])
    following = lax.ppermute(mine[:, TAPS:], "space", to_previous)
    summed = swap(sum_and_copy(swap(dw.reshape(16, OWN, CIN), "space")), "space")
    output = (own + came).astype(BF16).reshape(B, 32, 1, 256)
    input_grad = input_grad_local(mine, other, following).reshape(B, CIN, 2, 128)
    summed, input_grad = lax.optimization_barrier((summed, input_grad))
    kernel_grad = summed.reshape(ROWS, CIN)[:864].astype(F32).reshape(3, 3, 3, 32, CIN)
    return (output, input_grad, kernel_grad)


def solution(mesh):
    return jax.shard_map(
        body,
        mesh=mesh,
        in_specs=(
            P(None, None, "space", None),
            P(None, None, None, "filt", None),
            P(None, "filt", "space", None),
        ),
        out_specs=(
            P(None, "filt", "space", None),
            P(None, None, "space", "filt"),
            P(None, None, None, "filt", None),
        ),
        check_vma=False,
    )
```

```python
import jax
import jax.numpy as jnp
from jax import lax
from jax.experimental import pallas as pl
from jax.experimental.pallas import tpu as pltpu
from jax.sharding import PartitionSpec as P

B = 4
CIN = 128
EDGE = 32
HALF = 16
F32 = jnp.float32
BF16 = jnp.bfloat16
NT = (((1,), (1,)), ((), ()))
FULL = 63_000_000
TAPS = 14
PACKED = TAPS + 2
HELD = 432


def iota(shape, axis):
    return lax.broadcasted_iota(jnp.int32, shape, axis)


def columns(plane):
    parts = []
    for j in range(3):
        for k in range(3):
            parts.append(jnp.concatenate([plane(k, 2 * q + j) for q in range(HALF)], 0))
    return jnp.concatenate(parts, 1)


def conv_kernel(vol_ref, ker_ref, g_ref, own_ref, send_ref, odd_ref, keep_ref, go_ref,
                total, raw, arrived, ker_in, grads_in, perm, select, planes, cols):
    step = pl.program_id(0)

    def fetch(b):
        return pltpu.make_async_copy(vol_ref.at[b], raw.at[b], arrived.at[b])

    others = [
        pltpu.make_async_copy(ker_ref, ker_in, arrived.at[B]),
        pltpu.make_async_copy(g_ref, grads_in, arrived.at[B + 1]),
    ]

    @pl.when(step == 0)
    def _():
        fetch(0).start()
        for copy in others:
            copy.start()
        for b in range(1, B):
            fetch(b).start()

    @pl.when(step == 0)
    def _():
        row, col = iota((256, 256), 0), iota((256, 256), 1)
        source = (row & 15) * 16 + ((row >> 4) & 7) * 2 + (row >> 7)
        perm[...] = jnp.where(col == source, 1.0, 0.0).astype(BF16)
        row, col = iota((192, 128), 0), iota((192, 128), 1)
        depth = (row & 15) * 2 + (row >> 6) - 1
        wanted = (col == ((row >> 4) & 3) * 32 + depth) & (depth >= 0)
        select[...] = jnp.where(wanted, 1.0, 0.0).astype(BF16)
        total[...] = jnp.zeros_like(total)
        for k in range(3):
            planes[k, 0] = jnp.zeros((HALF, CIN), BF16)

    fetch(step).wait()
    wide = jnp.concatenate([raw[step, g * 256:(g + 1) * 256] for g in range(8)], 1)
    moved = jnp.dot(perm[...], wide, preferred_element_type=F32).astype(BF16)
    for lt in range(8):
        for x in range(2):
            start = (x * 8 + lt) * 16
            for g in range(8):
                cols[lt, x * 128 + g * 16:x * 128 + g * 16 + 16, :] = (
                    moved[start:start + 16, g * 128:(g + 1) * 128]
                )
    for k in range(3):
        odd_ref[0, k, 0] = jnp.zeros((HALF, CIN), BF16)
    for lt in range(8):
        turned = lax.dot_general(select[...], cols[lt], NT, preferred_element_type=F32).astype(BF16)
        for k in range(3):
            for y in range(4):
                start = k * 64 + y * 16
                planes[k, 1 + 4 * lt + y] = turned[start:start + 16, :128]
                odd_ref[0, k, 1 + 4 * lt + y] = turned[start:start + 16, 128:]

    @pl.when(step == 0)
    def _():
        for copy in others:
            copy.wait()

    def weights(i):
        return jnp.concatenate([ker_in[i * 9 + t] for t in range(9)], 1)

    grad = grads_in[step]
    even = columns(lambda k, y: planes[k, y])
    here = lax.dot_general(weights(1), even, NT, preferred_element_type=F32)
    back_even = jnp.dot(grad, even, preferred_element_type=F32)
    odd = columns(lambda k, y: odd_ref[0, k, y])
    both = lax.dot_general(
        jnp.concatenate([weights(2), weights(0)], 0), odd, NT, preferred_element_type=F32
    )
    back_odd = jnp.dot(grad, odd, preferred_element_type=F32)
    own_ref[0] = here + both[:32]
    send_ref[0] = both[32:]
    for t in range(9):
        lanes = slice(t * 128, (t + 1) * 128)
        total[t * 32:(t + 1) * 32] += back_even[:, lanes]
        total[(9 + t) * 32:(10 + t) * 32] += back_odd[:, lanes]

    @pl.when(step == B - 1)
    def _():
        first = lax.rem(lax.axis_index("space"), 2) == 0
        for chosen, low_ref, high_ref in ((first, keep_ref, go_ref), (~first, go_ref, keep_ref)):

            @pl.when(chosen)
            def _():
                low_ref[:288] = jnp.zeros((288, CIN), F32)
                low_ref[288:] = total[:144]
                high_ref[...] = total[144:]


def conv_local(vol, ker, g):
    per_sample = lambda *shape: pl.BlockSpec((1,) + shape, lambda b: (b,) + (0,) * len(shape))
    whole = lambda *shape: pl.BlockSpec(shape, lambda b: (0,) * len(shape))
    return pl.pallas_call(
        conv_kernel,
        grid=(B,),
        in_specs=[pl.BlockSpec(memory_space=pltpu.HBM)] * 3,
        out_specs=[per_sample(32, 256), per_sample(32, 256), per_sample(3, EDGE + 1, HALF, CIN), whole(HELD, CIN), whole(HELD, CIN)],
        out_shape=[
            jax.ShapeDtypeStruct((B, 32, 256), F32),
            jax.ShapeDtypeStruct((B, 32, 256), F32),
            jax.ShapeDtypeStruct((B, 3, EDGE + 1, HALF, CIN), BF16),
            jax.ShapeDtypeStruct((HELD, CIN), F32),
            jax.ShapeDtypeStruct((HELD, CIN), F32),
        ],
        scratch_shapes=[
            pltpu.VMEM((576, CIN), F32),
            pltpu.VMEM((B, 2048, 128), BF16),
            pltpu.SemaphoreType.DMA((B + 2,)),
            pltpu.VMEM((27, 32, CIN), BF16),
            pltpu.VMEM((B, 32, 256), BF16),
            pltpu.VMEM((256, 256), BF16),
            pltpu.VMEM((192, 128), BF16),
            pltpu.VMEM((3, EDGE + 1, HALF, CIN), BF16),
            pltpu.VMEM((8, 256, 128), BF16),
        ],
        compiler_params=pltpu.CompilerParams(vmem_limit_bytes=FULL),
        cost_estimate=pl.CostEstimate(flops=6_000_000_000, bytes_accessed=4_000_000, transcendentals=0),
        name="conv_local",
    )(vol, ker, g)


def next_kernel(odd_ref, gn_ref, _, __, keep_ref, go_ref, odd, grad, low, arrived):
    copies = [pltpu.make_async_copy(gn_ref, grad, arrived.at[B])]
    for b in range(B):
        copies.append(pltpu.make_async_copy(odd_ref.at[b], odd.at[b], arrived.at[b]))
    for copy in copies:
        copy.start()
    copies[0].wait()
    total = None
    for b in range(B):
        copies[1 + b].wait()
        back = jnp.dot(
            grad[b], columns(lambda k, y: odd[b, k, y]), preferred_element_type=F32
        )
        total = back if total is None else total + back
    for t in range(9):
        low[t * 32:(t + 1) * 32] = total[:, t * 128:(t + 1) * 128]
    first = lax.rem(lax.axis_index("space"), 2) == 0
    for chosen, ref in ((first, keep_ref), (~first, go_ref)):

        @pl.when(chosen)
        def _():
            last = pltpu.make_async_copy(low, ref.at[pl.ds(0, 288)], arrived.at[B + 1])
            last.start()
            last.wait()


def next_local(odd, gn, keep, go):
    return pl.pallas_call(
        next_kernel,
        in_specs=[pl.BlockSpec(memory_space=pltpu.HBM)] * 4,
        out_specs=[pl.BlockSpec(memory_space=pltpu.HBM)] * 2,
        out_shape=[jax.ShapeDtypeStruct((HELD, CIN), F32)] * 2,
        scratch_shapes=[
            pltpu.VMEM((B, 3, EDGE + 1, HALF, CIN), BF16),
            pltpu.VMEM((B, 32, 256), BF16),
            pltpu.VMEM((288, CIN), F32),
            pltpu.SemaphoreType.DMA((B + 2,)),
        ],
        input_output_aliases={2: 0, 3: 1},
        compiler_params=pltpu.CompilerParams(vmem_limit_bytes=FULL),
        cost_estimate=pl.CostEstimate(flops=1_000_000_000, bytes_accessed=2_000_000, transcendentals=0),
        name="next_local",
    )(odd, gn, keep, go)


def pack_kernel(ker_ref, g_ref, out_ref, half, grad, cells, sent):
    core = lax.rem(lax.axis_index("space"), 2)
    fetch_half = pltpu.make_async_copy(ker_ref.at[pl.ds(core * 13, TAPS)], half, sent.at[8])
    fetch_grad = pltpu.make_async_copy(g_ref, grad, sent.at[9])
    fetch_half.start()
    fetch_grad.start()
    fetch_half.wait()
    copies = [
        pltpu.make_async_copy(half, out_ref.at[f, pl.ds(0, TAPS)], sent.at[f])
        for f in range(8)
    ]
    for copy in copies:
        copy.start()
    fetch_grad.wait()
    for b in range(B):
        whole = jnp.concatenate([grad[b], jnp.zeros((32, 128), BF16)], 1)
        lane = (b % 2) * 64
        for f in range(8):
            cells[f, b // 2, :, lane:lane + 64] = whole[:, 32 * f:32 * f + 64]
    last = pltpu.make_async_copy(cells, out_ref.at[:, pl.ds(TAPS, 2)], sent.at[10])
    last.start()
    for copy in copies:
        copy.wait()
    last.wait()


def pack(ker, g):
    return pl.pallas_call(
        pack_kernel,
        in_specs=[pl.BlockSpec(memory_space=pltpu.HBM)] * 2,
        out_specs=pl.BlockSpec(memory_space=pltpu.HBM),
        out_shape=jax.ShapeDtypeStruct((8, PACKED, 32, 128), BF16),
        scratch_shapes=[
            pltpu.VMEM((TAPS, 32, CIN), BF16),
            pltpu.VMEM((B, 32, 256), BF16),
            pltpu.VMEM((8, 2, 32, 128), BF16),
            pltpu.SemaphoreType.DMA((11,)),
        ],
        compiler_params=pltpu.CompilerParams(vmem_limit_bytes=FULL),
        name="pack",
    )(ker, g)


def input_grad_kernel(mine_ref, other_ref, next_ref, out_ref, halves, grads, mixed, paired):
    core = lax.rem(lax.axis_index("space"), 2)
    halves[core] = mine_ref[:, :TAPS]
    halves[1 - core] = other_ref[:, :TAPS]
    last = (iota((128, 256), 0) & 15) == 15
    for p, (ref, first) in enumerate(((mine_ref, TAPS), (next_ref, 0))):
        for two in range(B // 2):
            block = ref[:, first + two].reshape(256, 128).astype(F32)
            turned = jnp.transpose(block)
            later = jnp.where(last, 0.0, pltpu.roll(turned, 127, 0))
            for shift, value in enumerate((turned, later)):
                low = value.astype(BF16)
                for b in range(2):
                    for q in range(3):
                        start = b * 64 + q * 16
                        grads[p, shift, q, 2 * two + b] = low[start:start + 16]

    def lhs(p, qs, rs):
        rows = [grads[p, rs, qs + q, b] for q in range(2) for b in range(B)]
        return jnp.concatenate(rows, 0)

    def tap(i, j, k):
        t = i * 9 + j * 3 + k
        half, place = (0, t) if t < TAPS else (1, t - 13)
        return halves[half, :, place].reshape(256, CIN)

    choices = (((1, 0),), ((2, 0), (0, 1)))
    for py in range(2):
        for pz in range(2):
            total = jnp.zeros((128, 256), F32)
            extra = jnp.zeros((128, 128), F32)
            for j, qs in choices[py]:
                for k, rs in choices[pz]:
                    two = jnp.concatenate([tap(1, j, k), tap(2, j, k)], 1)
                    total += jnp.dot(lhs(0, qs, rs), two, preferred_element_type=F32)
                    extra += jnp.dot(lhs(1, qs, rs), tap(0, j, k), preferred_element_type=F32)
            values = (total[:, :128], total[:, 128:] + extra)
            for px in range(2):
                for q in range(2):
                    for b in range(B):
                        start = (q * B + b) * 16
                        mixed[px, b, pl.ds((2 * q + py) * 32 + pz, 16, stride=2), :] = (
                            values[px][start:start + 16]
                        )
    for b in range(B):
        for px in range(2):
            paired[b, pl.ds(px, CIN, stride=2), :] = jnp.transpose(mixed[px, b])
        out_ref[b] = paired[b].astype(BF16)


def input_grad_local(mine, other, following):
    return pl.pallas_call(
        input_grad_kernel,
        out_shape=jax.ShapeDtypeStruct((B, 2 * CIN, 128), BF16),
        scratch_shapes=[
            pltpu.VMEM((2, 8, TAPS, 32, CIN), BF16),
            pltpu.VMEM((2, 2, 3, B, HALF, 256), BF16),
            pltpu.VMEM((2, B, 128, CIN), F32),
            pltpu.VMEM((B, 2 * CIN, 128), F32),
        ],
        compiler_params=pltpu.CompilerParams(vmem_limit_bytes=24 * 1024 * 1024),
        cost_estimate=pl.CostEstimate(flops=2_000_000_000, bytes_accessed=3_000_000, transcendentals=0),
        name="input_grad_local",
    )(mine, other, following)


SMALL = pltpu.CompilerParams(vmem_limit_bytes=4 * 1024 * 1024)


def place_kernel(mine_ref, theirs_ref, out_ref):
    core = lax.rem(lax.axis_index("space"), 2)
    out_ref[pl.ds(pl.multiple_of(core * HELD, 8), HELD)] = mine_ref[...]
    out_ref[pl.ds(pl.multiple_of((1 - core) * HELD, 8), HELD)] = theirs_ref[...]


def place(mine, theirs):
    return pl.pallas_call(
        place_kernel,
        out_shape=jax.ShapeDtypeStruct((2 * HELD, CIN), F32),
        compiler_params=SMALL,
        name="place",
    )(mine, theirs)


def swap(values, axis):
    return lax.all_to_all(values, axis, split_axis=0, concat_axis=0, tiled=True)


def body(volume, kernel, out_grad):
    spaces = lax.axis_size("space")
    g = out_grad.reshape(B, 32, 256)
    ker = kernel.reshape(27, 32, CIN)
    to_previous = [(i + 1, i) for i in range(spaces - 1)]
    to_next = [(i, i + 1) for i in range(spaces - 1)]
    g_next = lax.ppermute(g, "space", to_previous)
    packed = pack(ker, g)
    vol = volume.reshape(B, CIN, 2, 8, 128).transpose(0, 1, 3, 2, 4).reshape(B, 2048, 128)
    mine = swap(packed, "filt")
    own, send, odd, keep, go = conv_local(vol, ker, g)
    keep, go = next_local(odd, g_next, keep, go)
    keep, go, mine = lax.optimization_barrier((keep, go, mine))

    def exchange(values, bits):
        return lax.ppermute(values, "space", [(i, i ^ bits) for i in range(spaces)])

    came = lax.ppermute(send, "space", to_next)
    other = exchange(mine, 1)
    following = lax.ppermute(mine[:, TAPS:], "space", to_previous)
    pair = (keep + exchange(go, 1)).astype(BF16)
    pair, following = lax.optimization_barrier((pair, following))
    four = (pair.astype(F32) + exchange(pair, 8).astype(F32)).astype(BF16)
    parts = [exchange(four, bits) for bits in (2, 4, 6)]
    input_grad = input_grad_local(mine, other, following).reshape(B, CIN, 2, 128)
    parts, input_grad = lax.optimization_barrier((parts, input_grad))
    near, far, farther = (part.astype(F32) for part in parts)
    held = (four.astype(F32) + near) + (far + farther)
    kernel_grad = place(held, exchange(held, 1)).reshape(3, 3, 3, 32, CIN)
    output = (own + came).astype(BF16).reshape(B, 32, 1, 256)
    return (output, input_grad, kernel_grad)


def solution(mesh):
    return jax.shard_map(
        body,
        mesh=mesh,
        in_specs=(
            P(None, None, "space", None),
            P(None, None, None, "filt", None),
            P(None, "filt", "space", None),
        ),
        out_specs=(
            P(None, "filt", "space", None),
            P(None, None, "space", "filt"),
            P(None, None, None, "filt", None),
        ),
        check_vma=False,
    )
```

```python
import jax
import jax.numpy as jnp
from jax import lax
from jax.experimental import pallas as pl
from jax.experimental.pallas import tpu as pltpu
from jax.sharding import PartitionSpec as P

B = 4
CIN = 128
EDGE = 32
HALF = 16
F32 = jnp.float32
BF16 = jnp.bfloat16
NT = (((1,), (1,)), ((), ()))
FULL = 63_000_000
TAPS = 14
PACKED = TAPS + 4
HELD = 432


def iota(shape, axis):
    return lax.broadcasted_iota(jnp.int32, shape, axis)


def cut_cells(grad, cells):
    for b in range(B):
        whole = jnp.concatenate([grad[b], jnp.zeros((32, 128), BF16)], 1)
        lane = (b % 2) * 64
        for f in range(8):
            cells[f, b // 2, :, lane:lane + 64] = whole[:, 32 * f:32 * f + 64]


def prepare_kernel(vol_ref, ker_ref, g_ref, planes_ref, packed_ref,
                   raw, arrived, taps, grad, cells, sent, perm, select, cols):
    step = pl.program_id(0)
    core = lax.rem(lax.axis_index("space"), 2)

    def fetch(b):
        return pltpu.make_async_copy(vol_ref.at[b], raw.at[b], arrived.at[b])

    fetch_taps = pltpu.make_async_copy(ker_ref.at[pl.ds(core * 13, TAPS)], taps, arrived.at[B])
    fetch_grad = pltpu.make_async_copy(g_ref, grad, arrived.at[B + 1])
    copies = [
        pltpu.make_async_copy(taps, packed_ref.at[f, pl.ds(0, TAPS)], sent.at[f]) for f in range(8)
    ]
    copies.append(pltpu.make_async_copy(cells, packed_ref.at[:, pl.ds(TAPS, 2)], sent.at[8]))

    @pl.when(step == 0)
    def _():
        fetch(0).start()
        fetch_taps.start()
        fetch_grad.start()
        for b in range(1, B):
            fetch(b).start()
        row, col = iota((256, 256), 0), iota((256, 256), 1)
        source = (row & 15) * 16 + ((row >> 4) & 7) * 2 + (row >> 7)
        perm[...] = jnp.where(col == source, 1.0, 0.0).astype(BF16)
        row, col = iota((192, 128), 0), iota((192, 128), 1)
        depth = (row & 15) * 2 + (row >> 6) - 1
        wanted = (col == ((row >> 4) & 3) * 32 + depth) & (depth >= 0)
        select[...] = jnp.where(wanted, 1.0, 0.0).astype(BF16)

    @pl.when(step == 1)
    def _():
        fetch_taps.wait()
        for copy in copies[:8]:
            copy.start()
        fetch_grad.wait()
        cut_cells(grad, cells)
        copies[8].start()

    fetch(step).wait()
    wide = jnp.concatenate([raw[step, g * 256:(g + 1) * 256] for g in range(8)], 1)
    moved = jnp.dot(perm[...], wide, preferred_element_type=F32).astype(BF16)
    for lt in range(8):
        for x in range(2):
            start = (x * 8 + lt) * 16
            for g in range(8):
                cols[lt, x * 128 + g * 16:x * 128 + g * 16 + 16, :] = (
                    moved[start:start + 16, g * 128:(g + 1) * 128]
                )
    for x in range(2):
        for k in range(3):
            planes_ref[0, x, k, 0] = jnp.zeros((HALF, CIN), BF16)
    for lt in range(8):
        turned = lax.dot_general(select[...], cols[lt], NT, preferred_element_type=F32).astype(BF16)
        for k in range(3):
            for y in range(4):
                start = k * 64 + y * 16
                for x in range(2):
                    planes_ref[0, x, k, 1 + 4 * lt + y] = (
                        turned[start:start + 16, x * 128:(x + 1) * 128]
                    )

    @pl.when(step == B - 1)
    def _():
        for copy in copies:
            copy.wait()


def per_sample(*shape):
    return pl.BlockSpec((1,) + shape, lambda b: (b,) + (0,) * len(shape))


def whole_array(*shape):
    return pl.BlockSpec(shape, lambda b: (0,) * len(shape))


def prepare(vol, ker, g):
    return pl.pallas_call(
        prepare_kernel,
        grid=(B,),
        in_specs=[pl.BlockSpec(memory_space=pltpu.HBM)] * 3,
        out_specs=[per_sample(2, 3, EDGE + 1, HALF, CIN), pl.BlockSpec(memory_space=pltpu.HBM)],
        out_shape=[
            jax.ShapeDtypeStruct((B, 2, 3, EDGE + 1, HALF, CIN), BF16),
            jax.ShapeDtypeStruct((8, PACKED, 32, 128), BF16),
        ],
        scratch_shapes=[
            pltpu.VMEM((B, 2048, 128), BF16),
            pltpu.SemaphoreType.DMA((B + 2,)),
            pltpu.VMEM((TAPS, 32, CIN), BF16),
            pltpu.VMEM((B, 32, 256), BF16),
            pltpu.VMEM((8, 2, 32, 128), BF16),
            pltpu.SemaphoreType.DMA((9,)),
            pltpu.VMEM((256, 256), BF16),
            pltpu.VMEM((192, 128), BF16),
            pltpu.VMEM((8, 256, 128), BF16),
        ],
        compiler_params=pltpu.CompilerParams(vmem_limit_bytes=FULL),
        cost_estimate=pl.CostEstimate(flops=4_000_000_000, bytes_accessed=5_000_000, transcendentals=0),
        name="prepare",
    )(vol, ker, g)


def next_cells_kernel(gn_ref, _, packed_ref, cells, sent):
    cut_cells(gn_ref, cells)
    copy = pltpu.make_async_copy(cells, packed_ref.at[:, pl.ds(TAPS + 2, 2)], sent)
    copy.start()
    copy.wait()


def next_cells(gn, packed):
    return pl.pallas_call(
        next_cells_kernel,
        in_specs=[pl.BlockSpec(memory_space=pltpu.VMEM), pl.BlockSpec(memory_space=pltpu.HBM)],
        out_specs=pl.BlockSpec(memory_space=pltpu.HBM),
        out_shape=jax.ShapeDtypeStruct((8, PACKED, 32, 128), BF16),
        scratch_shapes=[pltpu.VMEM((8, 2, 32, 128), BF16), pltpu.SemaphoreType.DMA],
        input_output_aliases={1: 0},
        compiler_params=pltpu.CompilerParams(vmem_limit_bytes=FULL),
        name="next_cells",
    )(gn, packed)


def columns(plane):
    parts = []
    for j in range(3):
        for k in range(3):
            parts.append(jnp.concatenate([plane(k, 2 * q + j) for q in range(HALF)], 0))
    return jnp.concatenate(parts, 1)


def conv_kernel(planes_ref, ker_ref, g_ref, gn_ref, own_ref, send_ref, keep_ref, go_ref,
                total):
    step = pl.program_id(0)

    @pl.when(step == 0)
    def _():
        total[...] = jnp.zeros_like(total)

    def weights(i):
        return jnp.concatenate([ker_ref[i * 9 + t] for t in range(9)], 1)

    grad = g_ref[0]
    pair = jnp.concatenate([grad, gn_ref[0]], 0)
    even = columns(lambda k, y: planes_ref[0, 0, k, y])
    here = lax.dot_general(weights(1), even, NT, preferred_element_type=F32)
    back_even = jnp.dot(grad, even, preferred_element_type=F32)
    odd = columns(lambda k, y: planes_ref[0, 1, k, y])
    both = lax.dot_general(
        jnp.concatenate([weights(2), weights(0)], 0), odd, NT, preferred_element_type=F32
    )
    back_odd = jnp.dot(pair, odd, preferred_element_type=F32)
    own_ref[0] = here + both[:32]
    send_ref[0] = both[32:]
    for t in range(9):
        lanes = slice(t * 128, (t + 1) * 128)
        total[t * 32:(t + 1) * 32] += back_odd[32:, lanes]
        total[(9 + t) * 32:(10 + t) * 32] += back_even[:, lanes]
        total[(18 + t) * 32:(19 + t) * 32] += back_odd[:32, lanes]

    @pl.when(step == B - 1)
    def _():
        core = lax.rem(lax.axis_index("space"), 2)
        keep_ref[...] = total[pl.ds(pl.multiple_of(core * HELD, 8), HELD)]
        go_ref[...] = total[pl.ds(pl.multiple_of((1 - core) * HELD, 8), HELD)]


def conv_local(planes, ker, g, gn):
    return pl.pallas_call(
        conv_kernel,
        grid=(B,),
        in_specs=[
            per_sample(2, 3, EDGE + 1, HALF, CIN), whole_array(27, 32, CIN),
            per_sample(32, 256), per_sample(32, 256),
        ],
        out_specs=[
            per_sample(32, 256), per_sample(32, 256), whole_array(HELD, CIN), whole_array(HELD, CIN)
        ],
        out_shape=[
            jax.ShapeDtypeStruct((B, 32, 256), F32),
            jax.ShapeDtypeStruct((B, 32, 256), F32),
            jax.ShapeDtypeStruct((HELD, CIN), F32),
            jax.ShapeDtypeStruct((HELD, CIN), F32),
        ],
        scratch_shapes=[pltpu.VMEM((2 * HELD, CIN), F32)],
        compiler_params=pltpu.CompilerParams(vmem_limit_bytes=FULL),
        cost_estimate=pl.CostEstimate(flops=4_000_000_000, bytes_accessed=5_000_000, transcendentals=0),
        name="conv_local",
    )(planes, ker, g, gn)


def input_grad_kernel(mine_ref, other_ref, out_ref, halves, grads, mixed, paired):
    core = lax.rem(lax.axis_index("space"), 2)
    halves[core] = mine_ref[:, :TAPS]
    halves[1 - core] = other_ref[:, :TAPS]
    last = (iota((128, 256), 0) & 15) == 15
    for p in range(2):
        for two in range(B // 2):
            block = mine_ref[:, TAPS + 2 * p + two].reshape(256, 128).astype(F32)
            turned = jnp.transpose(block)
            later = jnp.where(last, 0.0, pltpu.roll(turned, 127, 0))
            for shift, value in enumerate((turned, later)):
                low = value.astype(BF16)
                for b in range(2):
                    for q in range(3):
                        start = b * 64 + q * 16
                        grads[p, shift, q, 2 * two + b] = low[start:start + 16]

    def lhs(p, qs, rs):
        rows = [grads[p, rs, qs + q, b] for q in range(2) for b in range(B)]
        return jnp.concatenate(rows, 0)

    def tap(i, j, k):
        t = i * 9 + j * 3 + k
        half, place = (0, t) if t < TAPS else (1, t - 13)
        return halves[half, :, place].reshape(256, CIN)

    choices = (((1, 0),), ((2, 0), (0, 1)))
    for py in range(2):
        for pz in range(2):
            total = jnp.zeros((128, 256), F32)
            extra = jnp.zeros((128, 128), F32)
            for j, qs in choices[py]:
                for k, rs in choices[pz]:
                    two = jnp.concatenate([tap(1, j, k), tap(2, j, k)], 1)
                    total += jnp.dot(lhs(0, qs, rs), two, preferred_element_type=F32)
                    extra += jnp.dot(lhs(1, qs, rs), tap(0, j, k), preferred_element_type=F32)
            values = (total[:, :128], total[:, 128:] + extra)
            for px in range(2):
                for q in range(2):
                    for b in range(B):
                        start = (q * B + b) * 16
                        mixed[px, b, pl.ds((2 * q + py) * 32 + pz, 16, stride=2), :] = (
                            values[px][start:start + 16]
                        )
    for b in range(B):
        for px in range(2):
            paired[b, pl.ds(px, CIN, stride=2), :] = jnp.transpose(mixed[px, b])
        out_ref[b] = paired[b].astype(BF16)


def input_grad_local(mine, other):
    return pl.pallas_call(
        input_grad_kernel,
        out_shape=jax.ShapeDtypeStruct((B, 2 * CIN, 128), BF16),
        scratch_shapes=[
            pltpu.VMEM((2, 8, TAPS, 32, CIN), BF16),
            pltpu.VMEM((2, 2, 3, B, HALF, 256), BF16),
            pltpu.VMEM((2, B, 128, CIN), F32),
            pltpu.VMEM((B, 2 * CIN, 128), F32),
        ],
        compiler_params=pltpu.CompilerParams(vmem_limit_bytes=24 * 1024 * 1024),
        cost_estimate=pl.CostEstimate(flops=2_000_000_000, bytes_accessed=3_000_000, transcendentals=0),
        name="input_grad_local",
    )(mine, other)


SMALL = pltpu.CompilerParams(vmem_limit_bytes=4 * 1024 * 1024)


def place_kernel(mine_ref, theirs_ref, out_ref):
    core = lax.rem(lax.axis_index("space"), 2)
    out_ref[pl.ds(pl.multiple_of(core * HELD, 8), HELD)] = mine_ref[...]
    out_ref[pl.ds(pl.multiple_of((1 - core) * HELD, 8), HELD)] = theirs_ref[...]


def place(mine, theirs):
    return pl.pallas_call(
        place_kernel,
        out_shape=jax.ShapeDtypeStruct((2 * HELD, CIN), F32),
        compiler_params=SMALL,
        name="place",
    )(mine, theirs)


def swap(values, axis):
    return lax.all_to_all(values, axis, split_axis=0, concat_axis=0, tiled=True)


def body(volume, kernel, out_grad):
    spaces = lax.axis_size("space")
    g = out_grad.reshape(B, 32, 256)
    ker = kernel.reshape(27, 32, CIN)
    to_previous = [(i + 1, i) for i in range(spaces - 1)]
    to_next = [(i, i + 1) for i in range(spaces - 1)]
    g_next = lax.ppermute(g, "space", to_previous)
    vol = volume.reshape(B, CIN, 2, 8, 128).transpose(0, 1, 3, 2, 4).reshape(B, 2048, 128)
    planes, packed = prepare(vol, ker, g)
    mine = swap(next_cells(g_next, packed), "filt")
    own, send, keep, go = conv_local(planes, ker, g, g_next)

    def exchange(values, bits):
        return lax.ppermute(values, "space", [(i, i ^ bits) for i in range(spaces)])

    came = lax.ppermute(send, "space", to_next)
    pair = (keep + exchange(go, 1)).astype(BF16)
    near, far, farther = (exchange(pair, bits).astype(F32) for bits in (2, 4, 6))
    row = ((pair.astype(F32) + near) + (far + farther)).astype(BF16)
    row, mine = lax.optimization_barrier((row, mine))
    other = exchange(mine, 1)
    across = exchange(row, 8)
    input_grad = input_grad_local(mine, other).reshape(B, CIN, 2, 128)
    across, input_grad = lax.optimization_barrier((across, input_grad))
    held = row.astype(F32) + across.astype(F32)
    kernel_grad = place(held, exchange(held, 1)).reshape(3, 3, 3, 32, CIN)
    output = (own + came).astype(BF16).reshape(B, 32, 1, 256)
    return (output, input_grad, kernel_grad)


def solution(mesh):
    return jax.shard_map(
        body,
        mesh=mesh,
        in_specs=(
            P(None, None, "space", None),
            P(None, None, None, "filt", None),
            P(None, "filt", "space", None),
        ),
        out_specs=(
            P(None, "filt", "space", None),
            P(None, None, "space", "filt"),
            P(None, None, None, "filt", None),
        ),
        check_vma=False,
    )
```

```python
import jax
import jax.numpy as jnp
from jax import lax
from jax.experimental import pallas as pl
from jax.experimental.pallas import tpu as pltpu
from jax.sharding import PartitionSpec as P

B = 4
CIN = 128
EDGE = 32
HALF = 16
F32 = jnp.float32
BF16 = jnp.bfloat16
NT = (((1,), (1,)), ((), ()))
FULL = 63_000_000
TAPS = 14
PACKED = TAPS + 4
HELD = 432


def iota(shape, axis):
    return lax.broadcasted_iota(jnp.int32, shape, axis)


def cut_cells(grad, cells):
    for b in range(B):
        whole = jnp.concatenate([grad[b], jnp.zeros((32, 128), BF16)], 1)
        lane = (b % 2) * 64
        for f in range(8):
            cells[f, b // 2, :, lane:lane + 64] = whole[:, 32 * f:32 * f + 64]


def prepare_kernel(vol_ref, ker_ref, g_ref, planes_ref, packed_ref,
                   raw, arrived, taps, grad, cells, sent, perm, select, cols, planes):
    core = lax.rem(lax.axis_index("space"), 2)
    fetches = [pltpu.make_async_copy(vol_ref.at[b], raw.at[b], arrived.at[b]) for b in range(B)]
    fetch_taps = pltpu.make_async_copy(ker_ref.at[pl.ds(core * 13, TAPS)], taps, arrived.at[B])
    fetch_grad = pltpu.make_async_copy(g_ref, grad, arrived.at[B + 1])
    copies = [
        pltpu.make_async_copy(taps, packed_ref.at[f, pl.ds(0, TAPS)], sent.at[f]) for f in range(8)
    ]
    copies.append(pltpu.make_async_copy(cells, packed_ref.at[:, pl.ds(TAPS, 2)], sent.at[8]))
    fetches[0].start()
    fetch_taps.start()
    fetch_grad.start()
    for b in range(1, B):
        fetches[b].start()
    row, col = iota((256, 256), 0), iota((256, 256), 1)
    source = (row & 15) * 16 + ((row >> 4) & 7) * 2 + (row >> 7)
    perm[...] = jnp.where(col == source, 1.0, 0.0).astype(BF16)
    row, col = iota((192, 128), 0), iota((192, 128), 1)
    depth = (row & 15) * 2 + (row >> 6) - 1
    wanted = (col == ((row >> 4) & 3) * 32 + depth) & (depth >= 0)
    select[...] = jnp.where(wanted, 1.0, 0.0).astype(BF16)

    for step in range(B):
        fetches[step].wait()
        wide = jnp.concatenate([raw[step, g * 256:(g + 1) * 256] for g in range(8)], 1)
        moved = jnp.dot(perm[...], wide, preferred_element_type=F32).astype(BF16)
        slot = step % 2
        for lt in range(8):
            for x in range(2):
                start = (x * 8 + lt) * 16
                for g in range(8):
                    cols[slot, lt, x * 128 + g * 16:x * 128 + g * 16 + 16, :] = (
                        moved[start:start + 16, g * 128:(g + 1) * 128]
                    )
        if step == 0:
            fetch_taps.wait()
            for copy in copies[:8]:
                copy.start()
            fetch_grad.wait()
            cut_cells(grad, cells)
            copies[8].start()
        for x in range(2):
            for k in range(3):
                planes[step, x, k, 0] = jnp.zeros((HALF, CIN), BF16)
        for lt in range(8):
            turned = lax.dot_general(
                select[...], cols[slot, lt], NT, preferred_element_type=F32
            ).astype(BF16)
            for k in range(3):
                for y in range(4):
                    start = k * 64 + y * 16
                    for x in range(2):
                        planes[step, x, k, 1 + 4 * lt + y] = (
                            turned[start:start + 16, x * 128:(x + 1) * 128]
                        )
        copies.append(pltpu.make_async_copy(planes.at[step], planes_ref.at[step], sent.at[9 + step]))
        copies[-1].start()
    for copy in copies:
        copy.wait()


def prepare(vol, ker, g):
    return pl.pallas_call(
        prepare_kernel,
        in_specs=[pl.BlockSpec(memory_space=pltpu.HBM)] * 3,
        out_specs=[pl.BlockSpec(memory_space=pltpu.HBM)] * 2,
        out_shape=[
            jax.ShapeDtypeStruct((B, 2, 3, EDGE + 1, HALF, CIN), BF16),
            jax.ShapeDtypeStruct((8, PACKED, 32, 128), BF16),
        ],
        scratch_shapes=[
            pltpu.VMEM((B, 2048, 128), BF16),
            pltpu.SemaphoreType.DMA((B + 2,)),
            pltpu.VMEM((TAPS, 32, CIN), BF16),
            pltpu.VMEM((B, 32, 256), BF16),
            pltpu.VMEM((8, 2, 32, 128), BF16),
            pltpu.SemaphoreType.DMA((9 + B,)),
            pltpu.VMEM((256, 256), BF16),
            pltpu.VMEM((192, 128), BF16),
            pltpu.VMEM((2, 8, 256, 128), BF16),
            pltpu.VMEM((B, 2, 3, EDGE + 1, HALF, CIN), BF16),
        ],
        compiler_params=pltpu.CompilerParams(vmem_limit_bytes=FULL),
        cost_estimate=pl.CostEstimate(flops=4_000_000_000, bytes_accessed=5_000_000, transcendentals=0),
        name="prepare",
    )(vol, ker, g)


def next_cells_kernel(gn_ref, _, packed_ref, cells, sent):
    cut_cells(gn_ref, cells)
    copy = pltpu.make_async_copy(cells, packed_ref.at[:, pl.ds(TAPS + 2, 2)], sent)
    copy.start()
    copy.wait()


def next_cells(gn, packed):
    return pl.pallas_call(
        next_cells_kernel,
        in_specs=[pl.BlockSpec(memory_space=pltpu.VMEM), pl.BlockSpec(memory_space=pltpu.HBM)],
        out_specs=pl.BlockSpec(memory_space=pltpu.HBM),
        out_shape=jax.ShapeDtypeStruct((8, PACKED, 32, 128), BF16),
        scratch_shapes=[pltpu.VMEM((8, 2, 32, 128), BF16), pltpu.SemaphoreType.DMA],
        input_output_aliases={1: 0},
        compiler_params=pltpu.CompilerParams(vmem_limit_bytes=FULL),
        name="next_cells",
    )(gn, packed)


def columns(plane):
    parts = []
    for j in range(3):
        for k in range(3):
            parts.append(jnp.concatenate([plane(k, 2 * q + j) for q in range(HALF)], 0))
    return jnp.concatenate(parts, 1)


def conv_kernel(planes_ref, ker_ref, g_ref, gn_ref, own_ref, send_ref, keep_ref, go_ref,
                planes, ker, grads, own, send, total, arrived, sent):
    fetch_planes = [
        pltpu.make_async_copy(planes_ref.at[b], planes.at[b], arrived.at[b]) for b in range(B)
    ]
    others = [
        pltpu.make_async_copy(ker_ref, ker, arrived.at[B]),
        pltpu.make_async_copy(g_ref, grads.at[0], arrived.at[B + 1]),
        pltpu.make_async_copy(gn_ref, grads.at[1], arrived.at[B + 2]),
    ]
    fetch_planes[0].start()
    for copy in others + fetch_planes[1:]:
        copy.start()

    def weights(i):
        return jnp.concatenate([ker[i * 9 + t] for t in range(9)], 1)

    for copy in others:
        copy.wait()
    for step in range(B):
        fetch_planes[step].wait()
        grad = grads[0, step]
        pair = jnp.concatenate([grad, grads[1, step]], 0)
        even = columns(lambda k, y: planes[step, 0, k, y])
        here = lax.dot_general(weights(1), even, NT, preferred_element_type=F32)
        back_even = jnp.dot(grad, even, preferred_element_type=F32)
        odd = columns(lambda k, y: planes[step, 1, k, y])
        both = lax.dot_general(
            jnp.concatenate([weights(2), weights(0)], 0), odd, NT, preferred_element_type=F32
        )
        back_odd = jnp.dot(pair, odd, preferred_element_type=F32)
        own[step] = here + both[:32]
        send[step] = both[32:]
        for t in range(9):
            lanes = slice(t * 128, (t + 1) * 128)
            for first, value in (
                (t, back_odd[32:, lanes]), (9 + t, back_even[:, lanes]), (18 + t, back_odd[:32, lanes])
            ):
                rows = slice(first * 32, first * 32 + 32)
                total[rows] = value if step == 0 else total[rows] + value
    core = lax.rem(lax.axis_index("space"), 2)
    halves = [
        total.at[pl.ds(pl.multiple_of(half * HELD, 8), HELD)] for half in (core, 1 - core)
    ]
    copies = [
        pltpu.make_async_copy(source, target, sent.at[i])
        for i, (source, target) in enumerate(zip([*halves, own, send], [keep_ref, go_ref, own_ref, send_ref]))
    ]
    for copy in copies:
        copy.start()
    for copy in copies:
        copy.wait()


def conv_local(planes, ker, g, gn):
    return pl.pallas_call(
        conv_kernel,
        in_specs=[pl.BlockSpec(memory_space=pltpu.HBM)] * 4,
        out_specs=[pl.BlockSpec(memory_space=pltpu.HBM)] * 4,
        out_shape=[
            jax.ShapeDtypeStruct((B, 32, 256), F32),
            jax.ShapeDtypeStruct((B, 32, 256), F32),
            jax.ShapeDtypeStruct((HELD, CIN), F32),
            jax.ShapeDtypeStruct((HELD, CIN), F32),
        ],
        scratch_shapes=[
            pltpu.VMEM((B, 2, 3, EDGE + 1, HALF, CIN), BF16),
            pltpu.VMEM((27, 32, CIN), BF16),
            pltpu.VMEM((2, B, 32, 256), BF16),
            pltpu.VMEM((B, 32, 256), F32),
            pltpu.VMEM((B, 32, 256), F32),
            pltpu.VMEM((2 * HELD, CIN), F32),
            pltpu.SemaphoreType.DMA((B + 3,)),
            pltpu.SemaphoreType.DMA((4,)),
        ],
        compiler_params=pltpu.CompilerParams(vmem_limit_bytes=FULL),
        cost_estimate=pl.CostEstimate(flops=4_000_000_000, bytes_accessed=5_000_000, transcendentals=0),
        name="conv_local",
    )(planes, ker, g, gn)


def input_grad_kernel(mine_ref, other_ref, out_ref, halves, grads, mixed, paired):
    core = lax.rem(lax.axis_index("space"), 2)
    halves[core] = mine_ref[:, :TAPS]
    halves[1 - core] = other_ref[:, :TAPS]
    last = (iota((128, 256), 0) & 15) == 15
    for p in range(2):
        for two in range(B // 2):
            block = mine_ref[:, TAPS + 2 * p + two].reshape(256, 128).astype(F32)
            turned = jnp.transpose(block)
            later = jnp.where(last, 0.0, pltpu.roll(turned, 127, 0))
            for shift, value in enumerate((turned, later)):
                low = value.astype(BF16)
                for b in range(2):
                    for q in range(3):
                        start = b * 64 + q * 16
                        grads[p, shift, q, 2 * two + b] = low[start:start + 16]

    def lhs(p, qs, rs):
        rows = [grads[p, rs, qs + q, b] for q in range(2) for b in range(B)]
        return jnp.concatenate(rows, 0)

    def tap(i, j, k):
        t = i * 9 + j * 3 + k
        half, place = (0, t) if t < TAPS else (1, t - 13)
        return halves[half, :, place].reshape(256, CIN)

    choices = (((1, 0),), ((2, 0), (0, 1)))
    for py in range(2):
        for pz in range(2):
            total = jnp.zeros((128, 256), F32)
            extra = jnp.zeros((128, 128), F32)
            for j, qs in choices[py]:
                for k, rs in choices[pz]:
                    two = jnp.concatenate([tap(1, j, k), tap(2, j, k)], 1)
                    total += jnp.dot(lhs(0, qs, rs), two, preferred_element_type=F32)
                    extra += jnp.dot(lhs(1, qs, rs), tap(0, j, k), preferred_element_type=F32)
            values = (total[:, :128], total[:, 128:] + extra)
            for px in range(2):
                for q in range(2):
                    for b in range(B):
                        start = (q * B + b) * 16
                        mixed[px, b, pl.ds((2 * q + py) * 32 + pz, 16, stride=2), :] = (
                            values[px][start:start + 16]
                        )
    for b in range(B):
        for px in range(2):
            paired[b, pl.ds(px, CIN, stride=2), :] = jnp.transpose(mixed[px, b])
        out_ref[b] = paired[b].astype(BF16)


def input_grad_local(mine, other):
    return pl.pallas_call(
        input_grad_kernel,
        out_shape=jax.ShapeDtypeStruct((B, 2 * CIN, 128), BF16),
        scratch_shapes=[
            pltpu.VMEM((2, 8, TAPS, 32, CIN), BF16),
            pltpu.VMEM((2, 2, 3, B, HALF, 256), BF16),
            pltpu.VMEM((2, B, 128, CIN), F32),
            pltpu.VMEM((B, 2 * CIN, 128), F32),
        ],
        compiler_params=pltpu.CompilerParams(vmem_limit_bytes=24 * 1024 * 1024),
        cost_estimate=pl.CostEstimate(flops=2_000_000_000, bytes_accessed=3_000_000, transcendentals=0),
        name="input_grad_local",
    )(mine, other)


SMALL = pltpu.CompilerParams(vmem_limit_bytes=4 * 1024 * 1024)


def place_kernel(mine_ref, theirs_ref, out_ref):
    core = lax.rem(lax.axis_index("space"), 2)
    out_ref[pl.ds(pl.multiple_of(core * HELD, 8), HELD)] = mine_ref[...]
    out_ref[pl.ds(pl.multiple_of((1 - core) * HELD, 8), HELD)] = theirs_ref[...]


def place(mine, theirs):
    return pl.pallas_call(
        place_kernel,
        out_shape=jax.ShapeDtypeStruct((2 * HELD, CIN), F32),
        compiler_params=SMALL,
        name="place",
    )(mine, theirs)


def swap(values, axis):
    return lax.all_to_all(values, axis, split_axis=0, concat_axis=0, tiled=True)


def body(volume, kernel, out_grad):
    spaces = lax.axis_size("space")
    g = out_grad.reshape(B, 32, 256)
    ker = kernel.reshape(27, 32, CIN)
    to_previous = [(i + 1, i) for i in range(spaces - 1)]
    to_next = [(i, i + 1) for i in range(spaces - 1)]
    g_next = lax.ppermute(g, "space", to_previous)
    vol = volume.reshape(B, CIN, 2, 8, 128).transpose(0, 1, 3, 2, 4).reshape(B, 2048, 128)
    planes, packed = prepare(vol, ker, g)
    mine = swap(next_cells(g_next, packed), "filt")
    own, send, keep, go = conv_local(planes, ker, g, g_next)

    def exchange(values, bits):
        return lax.ppermute(values, "space", [(i, i ^ bits) for i in range(spaces)])

    turn = spaces // 2
    relayed = lax.ppermute(send, "space", [(turn - 1, spaces - 1)])
    pair = (keep + exchange(go, 1)).astype(BF16)
    near, far, farther = (exchange(pair, bits).astype(F32) for bits in (4, 6, 2))
    row = ((pair.astype(F32) + near) + (far + farther)).astype(BF16)
    row, mine, relayed = lax.optimization_barrier((row, mine, relayed))
    passed = jnp.where(lax.axis_index("space") == spaces - 1, relayed, send)
    came = lax.ppermute(
        passed, "space", [(i, i + 1) for i in range(spaces - 1) if i != turn - 1] + [(spaces - 1, turn)]
    )
    other = exchange(mine, 1)
    across = exchange(row, 8)
    input_grad = input_grad_local(mine, other).reshape(B, CIN, 2, 128)
    across, input_grad = lax.optimization_barrier((across, input_grad))
    held = row.astype(F32) + across.astype(F32)
    kernel_grad = place(held, exchange(held, 1)).reshape(3, 3, 3, 32, CIN)
    output = (own + came).astype(BF16).reshape(B, 32, 1, 256)
    return (output, input_grad, kernel_grad)


def solution(mesh):
    return jax.shard_map(
        body,
        mesh=mesh,
        in_specs=(
            P(None, None, "space", None),
            P(None, None, None, "filt", None),
            P(None, "filt", "space", None),
        ),
        out_specs=(
            P(None, "filt", "space", None),
            P(None, None, "space", "filt"),
            P(None, None, None, "filt", None),
        ),
        check_vma=False,
    )
```

```python
import jax
import jax.numpy as jnp
from jax import lax
from jax.experimental import pallas as pl
from jax.experimental.pallas import tpu as pltpu
from jax.sharding import PartitionSpec as P

B = 4
CIN = 128
EDGE = 32
HALF = 16
F32 = jnp.float32
BF16 = jnp.bfloat16
NT = (((1,), (1,)), ((), ()))
FULL = 63_000_000
TAPS = 14
PACKED = TAPS + 4
HELD = 432


def iota(shape, axis):
    return lax.broadcasted_iota(jnp.int32, shape, axis)


def cut_cells(grad, cells):
    for b in range(B):
        whole = jnp.concatenate([grad[b], jnp.zeros((32, 128), BF16)], 1)
        lane = (b % 2) * 64
        for f in range(8):
            cells[f, b // 2, :, lane:lane + 64] = whole[:, 32 * f:32 * f + 64]


def prepare_kernel(vol_ref, ker_ref, g_ref, planes_ref, packed_ref,
                   raw, arrived, taps, grad, cells, sent, perm, select, cols, planes):
    core = lax.rem(lax.axis_index("space"), 2)
    fetches = [pltpu.make_async_copy(vol_ref.at[b], raw.at[b], arrived.at[b]) for b in range(B)]
    fetch_taps = pltpu.make_async_copy(ker_ref.at[pl.ds(core * 13, TAPS)], taps, arrived.at[B])
    fetch_grad = pltpu.make_async_copy(g_ref, grad, arrived.at[B + 1])
    copies = [
        pltpu.make_async_copy(taps, packed_ref.at[f, pl.ds(0, TAPS)], sent.at[f]) for f in range(8)
    ]
    copies.append(pltpu.make_async_copy(cells, packed_ref.at[:, pl.ds(TAPS, 2)], sent.at[8]))
    fetches[0].start()
    fetch_taps.start()
    fetch_grad.start()
    for b in range(1, B):
        fetches[b].start()
    row, col = iota((256, 256), 0), iota((256, 256), 1)
    source = (row & 15) * 16 + ((row >> 4) & 7) * 2 + (row >> 7)
    perm[...] = jnp.where(col == source, 1.0, 0.0).astype(BF16)
    row, col = iota((192, 128), 0), iota((192, 128), 1)
    depth = (row & 15) * 2 + (row >> 6) - 1
    wanted = (col == ((row >> 4) & 3) * 32 + depth) & (depth >= 0)
    select[...] = jnp.where(wanted, 1.0, 0.0).astype(BF16)

    for step in range(B):
        fetches[step].wait()
        wide = jnp.concatenate([raw[step, g * 256:(g + 1) * 256] for g in range(8)], 1)
        moved = jnp.dot(perm[...], wide, preferred_element_type=F32).astype(BF16)
        slot = step % 2
        for lt in range(8):
            for x in range(2):
                start = (x * 8 + lt) * 16
                for g in range(8):
                    cols[slot, lt, x * 128 + g * 16:x * 128 + g * 16 + 16, :] = (
                        moved[start:start + 16, g * 128:(g + 1) * 128]
                    )
        if step == 0:
            fetch_taps.wait()
            for copy in copies[:8]:
                copy.start()
            fetch_grad.wait()
            cut_cells(grad, cells)
            copies[8].start()
        for x in range(2):
            for k in range(3):
                planes[step, x, k, 0] = jnp.zeros((HALF, CIN), BF16)
        for lt in range(8):
            turned = lax.dot_general(
                select[...], cols[slot, lt], NT, preferred_element_type=F32
            ).astype(BF16)
            for k in range(3):
                for y in range(4):
                    start = k * 64 + y * 16
                    for x in range(2):
                        planes[step, x, k, 1 + 4 * lt + y] = (
                            turned[start:start + 16, x * 128:(x + 1) * 128]
                        )
        copies.append(pltpu.make_async_copy(planes.at[step], planes_ref.at[step], sent.at[9 + step]))
        copies[-1].start()
    for copy in copies:
        copy.wait()


def prepare(vol, ker, g):
    return pl.pallas_call(
        prepare_kernel,
        in_specs=[pl.BlockSpec(memory_space=pltpu.HBM)] * 3,
        out_specs=[pl.BlockSpec(memory_space=pltpu.HBM)] * 2,
        out_shape=[
            jax.ShapeDtypeStruct((B, 2, 3, EDGE + 1, HALF, CIN), BF16),
            jax.ShapeDtypeStruct((8, PACKED, 32, 128), BF16),
        ],
        scratch_shapes=[
            pltpu.VMEM((B, 2048, 128), BF16),
            pltpu.SemaphoreType.DMA((B + 2,)),
            pltpu.VMEM((TAPS, 32, CIN), BF16),
            pltpu.VMEM((B, 32, 256), BF16),
            pltpu.VMEM((8, 2, 32, 128), BF16),
            pltpu.SemaphoreType.DMA((9 + B,)),
            pltpu.VMEM((256, 256), BF16),
            pltpu.VMEM((192, 128), BF16),
            pltpu.VMEM((2, 8, 256, 128), BF16),
            pltpu.VMEM((B, 2, 3, EDGE + 1, HALF, CIN), BF16),
        ],
        compiler_params=pltpu.CompilerParams(vmem_limit_bytes=FULL),
        cost_estimate=pl.CostEstimate(flops=4_000_000_000, bytes_accessed=5_000_000, transcendentals=0),
        name="prepare",
    )(vol, ker, g)


def next_cells_kernel(gn_ref, _, packed_ref, cells, sent):
    cut_cells(gn_ref, cells)
    copy = pltpu.make_async_copy(cells, packed_ref.at[:, pl.ds(TAPS + 2, 2)], sent)
    copy.start()
    copy.wait()


def next_cells(gn, packed):
    return pl.pallas_call(
        next_cells_kernel,
        in_specs=[pl.BlockSpec(memory_space=pltpu.VMEM), pl.BlockSpec(memory_space=pltpu.HBM)],
        out_specs=pl.BlockSpec(memory_space=pltpu.HBM),
        out_shape=jax.ShapeDtypeStruct((8, PACKED, 32, 128), BF16),
        scratch_shapes=[pltpu.VMEM((8, 2, 32, 128), BF16), pltpu.SemaphoreType.DMA],
        input_output_aliases={1: 0},
        compiler_params=pltpu.CompilerParams(vmem_limit_bytes=FULL),
        name="next_cells",
    )(gn, packed)


def columns(plane):
    parts = []
    for j in range(3):
        for k in range(3):
            parts.append(jnp.concatenate([plane(k, 2 * q + j) for q in range(HALF)], 0))
    return jnp.concatenate(parts, 1)


def conv_kernel(planes_ref, ker_ref, g_ref, gn_ref, own_ref, send_ref, keep_ref, go_ref,
                planes, ker, grads, own, send, total, arrived, sent):
    fetch_planes = [
        pltpu.make_async_copy(planes_ref.at[b], planes.at[b], arrived.at[b]) for b in range(B)
    ]
    others = [
        pltpu.make_async_copy(ker_ref, ker, arrived.at[B]),
        pltpu.make_async_copy(g_ref, grads.at[0], arrived.at[B + 1]),
        pltpu.make_async_copy(gn_ref, grads.at[1], arrived.at[B + 2]),
    ]
    fetch_planes[0].start()
    for copy in others + fetch_planes[1:]:
        copy.start()

    def weights(i):
        return jnp.concatenate([ker[i * 9 + t] for t in range(9)], 1)

    for copy in others:
        copy.wait()
    for step in range(B):
        fetch_planes[step].wait()
        grad = grads[0, step]
        pair = jnp.concatenate([grad, grads[1, step]], 0)
        even = columns(lambda k, y: planes[step, 0, k, y])
        here = lax.dot_general(weights(1), even, NT, preferred_element_type=F32)
        back_even = jnp.dot(grad, even, preferred_element_type=F32)
        odd = columns(lambda k, y: planes[step, 1, k, y])
        both = lax.dot_general(
            jnp.concatenate([weights(2), weights(0)], 0), odd, NT, preferred_element_type=F32
        )
        back_odd = jnp.dot(pair, odd, preferred_element_type=F32)
        own[step] = here + both[:32]
        send[step] = both[32:]
        for t in range(9):
            lanes = slice(t * 128, (t + 1) * 128)
            for first, value in (
                (t, back_odd[32:, lanes]), (9 + t, back_even[:, lanes]), (18 + t, back_odd[:32, lanes])
            ):
                rows = slice(first * 32, first * 32 + 32)
                total[rows] = value if step == 0 else total[rows] + value
    core = lax.rem(lax.axis_index("space"), 2)
    halves = [
        total.at[pl.ds(pl.multiple_of(half * HELD, 8), HELD)] for half in (core, 1 - core)
    ]
    copies = [
        pltpu.make_async_copy(source, target, sent.at[i])
        for i, (source, target) in enumerate(zip([*halves, own, send], [keep_ref, go_ref, own_ref, send_ref]))
    ]
    for copy in copies:
        copy.start()
    for copy in copies:
        copy.wait()


def conv_local(planes, ker, g, gn):
    return pl.pallas_call(
        conv_kernel,
        in_specs=[pl.BlockSpec(memory_space=pltpu.HBM)] * 4,
        out_specs=[pl.BlockSpec(memory_space=pltpu.HBM)] * 4,
        out_shape=[
            jax.ShapeDtypeStruct((B, 32, 256), F32),
            jax.ShapeDtypeStruct((B, 32, 256), F32),
            jax.ShapeDtypeStruct((HELD, CIN), F32),
            jax.ShapeDtypeStruct((HELD, CIN), F32),
        ],
        scratch_shapes=[
            pltpu.VMEM((B, 2, 3, EDGE + 1, HALF, CIN), BF16),
            pltpu.VMEM((27, 32, CIN), BF16),
            pltpu.VMEM((2, B, 32, 256), BF16),
            pltpu.VMEM((B, 32, 256), F32),
            pltpu.VMEM((B, 32, 256), F32),
            pltpu.VMEM((2 * HELD, CIN), F32),
            pltpu.SemaphoreType.DMA((B + 3,)),
            pltpu.SemaphoreType.DMA((4,)),
        ],
        compiler_params=pltpu.CompilerParams(vmem_limit_bytes=FULL),
        cost_estimate=pl.CostEstimate(flops=4_000_000_000, bytes_accessed=5_000_000, transcendentals=0),
        name="conv_local",
    )(planes, ker, g, gn)


def input_grad_kernel(mine_ref, other_ref, out_ref, halves, grads, mixed, paired):
    core = lax.rem(lax.axis_index("space"), 2)
    halves[core] = mine_ref[:, :TAPS]
    halves[1 - core] = other_ref[:, :TAPS]
    last = (iota((128, 256), 0) & 15) == 15
    for p in range(2):
        for two in range(B // 2):
            block = mine_ref[:, TAPS + 2 * p + two].reshape(256, 128).astype(F32)
            turned = jnp.transpose(block)
            later = jnp.where(last, 0.0, pltpu.roll(turned, 127, 0))
            for shift, value in enumerate((turned, later)):
                low = value.astype(BF16)
                for b in range(2):
                    for q in range(3):
                        start = b * 64 + q * 16
                        grads[p, shift, q, 2 * two + b] = low[start:start + 16]

    def lhs(p, qs, rs):
        rows = [grads[p, rs, qs + q, b] for q in range(2) for b in range(B)]
        return jnp.concatenate(rows, 0)

    def tap(i, j, k):
        t = i * 9 + j * 3 + k
        half, place = (0, t) if t < TAPS else (1, t - 13)
        return halves[half, :, place].reshape(256, CIN)

    choices = (((1, 0),), ((2, 0), (0, 1)))
    for py in range(2):
        for pz in range(2):
            total = jnp.zeros((128, 256), F32)
            extra = jnp.zeros((128, 128), F32)
            for j, qs in choices[py]:
                for k, rs in choices[pz]:
                    two = jnp.concatenate([tap(1, j, k), tap(2, j, k)], 1)
                    total += jnp.dot(lhs(0, qs, rs), two, preferred_element_type=F32)
                    extra += jnp.dot(lhs(1, qs, rs), tap(0, j, k), preferred_element_type=F32)
            values = (total[:, :128], total[:, 128:] + extra)
            for px in range(2):
                for q in range(2):
                    for b in range(B):
                        start = (q * B + b) * 16
                        mixed[px, b, pl.ds((2 * q + py) * 32 + pz, 16, stride=2), :] = (
                            values[px][start:start + 16]
                        )
    for b in range(B):
        for px in range(2):
            paired[b, pl.ds(px, CIN, stride=2), :] = jnp.transpose(mixed[px, b])
        out_ref[b] = paired[b].astype(BF16)


def input_grad_local(mine, other):
    return pl.pallas_call(
        input_grad_kernel,
        out_shape=jax.ShapeDtypeStruct((B, 2 * CIN, 128), BF16),
        scratch_shapes=[
            pltpu.VMEM((2, 8, TAPS, 32, CIN), BF16),
            pltpu.VMEM((2, 2, 3, B, HALF, 256), BF16),
            pltpu.VMEM((2, B, 128, CIN), F32),
            pltpu.VMEM((B, 2 * CIN, 128), F32),
        ],
        compiler_params=pltpu.CompilerParams(vmem_limit_bytes=24 * 1024 * 1024),
        cost_estimate=pl.CostEstimate(flops=2_000_000_000, bytes_accessed=3_000_000, transcendentals=0),
        name="input_grad_local",
    )(mine, other)


SMALL = pltpu.CompilerParams(vmem_limit_bytes=4 * 1024 * 1024)


def place_kernel(mine_ref, theirs_ref, out_ref):
    core = lax.rem(lax.axis_index("space"), 2)
    out_ref[pl.ds(pl.multiple_of(core * HELD, 8), HELD)] = mine_ref[...]
    out_ref[pl.ds(pl.multiple_of((1 - core) * HELD, 8), HELD)] = theirs_ref[...]


def place(mine, theirs):
    return pl.pallas_call(
        place_kernel,
        out_shape=jax.ShapeDtypeStruct((2 * HELD, CIN), F32),
        compiler_params=SMALL,
        name="place",
    )(mine, theirs)


def swap(values, axis):
    return lax.all_to_all(values, axis, split_axis=0, concat_axis=0, tiled=True)


def body(volume, kernel, out_grad):
    spaces = lax.axis_size("space")
    g = out_grad.reshape(B, 32, 256)
    ker = kernel.reshape(27, 32, CIN)
    to_previous = [(i + 1, i) for i in range(spaces - 1)]
    to_next = [(i, i + 1) for i in range(spaces - 1)]
    g_next = lax.ppermute(g, "space", to_previous)
    vol = volume.reshape(B, CIN, 2, 8, 128).transpose(0, 1, 3, 2, 4).reshape(B, 2048, 128)
    planes, packed = prepare(vol, ker, g)
    mine = swap(next_cells(g_next, packed), "filt")
    own, send, keep, go = conv_local(planes, ker, g, g_next)

    def exchange(values, bits):
        return lax.ppermute(values, "space", [(i, i ^ bits) for i in range(spaces)])

    turn = spaces // 2
    relayed = lax.ppermute(send, "space", [(turn - 1, spaces - 1)])
    came = lax.ppermute(send, "space", [(i, i + 1) for i in range(spaces - 1) if i != turn - 1])
    pair = (keep + exchange(go, 1)).astype(BF16)
    near, far, farther = (exchange(pair, bits).astype(F32) for bits in (2, 6, 4))
    row = ((pair.astype(F32) + near) + (far + farther)).astype(BF16)
    row, mine, relayed, came = lax.optimization_barrier((row, mine, relayed, came))
    turned = lax.ppermute(relayed, "space", [(spaces - 1, turn)])
    other = exchange(mine, 1)
    across = exchange(row, 8)
    input_grad = input_grad_local(mine, other).reshape(B, CIN, 2, 128)
    across, input_grad = lax.optimization_barrier((across, input_grad))
    held = row.astype(F32) + across.astype(F32)
    kernel_grad = place(held, exchange(held, 1)).reshape(3, 3, 3, 32, CIN)
    output = (own + came + turned).astype(BF16).reshape(B, 32, 1, 256)
    return (output, input_grad, kernel_grad)


def solution(mesh):
    return jax.shard_map(
        body,
        mesh=mesh,
        in_specs=(
            P(None, None, "space", None),
            P(None, None, None, "filt", None),
            P(None, "filt", "space", None),
        ),
        out_specs=(
            P(None, "filt", "space", None),
            P(None, None, "space", "filt"),
            P(None, None, None, "filt", None),
        ),
        check_vma=False,
    )
```

```python
import jax
import jax.numpy as jnp
from jax import lax
from jax.experimental import pallas as pl
from jax.experimental.pallas import tpu as pltpu
from jax.sharding import PartitionSpec as P

B = 4
CIN = 128
EDGE = 32
HALF = 16
F32 = jnp.float32
BF16 = jnp.bfloat16
NT = (((1,), (1,)), ((), ()))
FULL = 63_000_000
TAPS = 14
PACKED = TAPS + 4
HELD = 432


def iota(shape, axis):
    return lax.broadcasted_iota(jnp.int32, shape, axis)


def cut_cells(grad, cells):
    for b in range(B):
        whole = jnp.concatenate([grad[b], jnp.zeros((32, 128), BF16)], 1)
        lane = (b % 2) * 64
        for f in range(8):
            cells[f, b // 2, :, lane:lane + 64] = whole[:, 32 * f:32 * f + 64]


def prepare_kernel(vol_ref, ker_ref, g_ref, planes_ref, packed_ref,
                   raw, arrived, taps, grad, cells, sent, perm, select, cols, planes):
    core = lax.rem(lax.axis_index("space"), 2)
    fetches = [pltpu.make_async_copy(vol_ref.at[b], raw.at[b], arrived.at[b]) for b in range(B)]
    fetch_taps = pltpu.make_async_copy(ker_ref.at[pl.ds(core * 13, TAPS)], taps, arrived.at[B])
    fetch_grad = pltpu.make_async_copy(g_ref, grad, arrived.at[B + 1])
    copies = [
        pltpu.make_async_copy(taps, packed_ref.at[f, pl.ds(0, TAPS)], sent.at[f]) for f in range(8)
    ]
    copies.append(pltpu.make_async_copy(cells, packed_ref.at[:, pl.ds(TAPS, 2)], sent.at[8]))
    fetches[0].start()
    fetch_taps.start()
    fetch_grad.start()
    for b in range(1, B):
        fetches[b].start()
    row, col = iota((256, 256), 0), iota((256, 256), 1)
    source = (row & 15) * 16 + ((row >> 4) & 7) * 2 + (row >> 7)
    perm[...] = jnp.where(col == source, 1.0, 0.0).astype(BF16)
    row, col = iota((192, 128), 0), iota((192, 128), 1)
    depth = (row & 15) * 2 + (row >> 6) - 1
    wanted = (col == ((row >> 4) & 3) * 32 + depth) & (depth >= 0)
    select[...] = jnp.where(wanted, 1.0, 0.0).astype(BF16)

    for step in range(B):
        fetches[step].wait()
        wide = jnp.concatenate([raw[step, g * 256:(g + 1) * 256] for g in range(8)], 1)
        moved = jnp.dot(perm[...], wide, preferred_element_type=F32).astype(BF16)
        slot = step % 2
        for lt in range(8):
            for x in range(2):
                start = (x * 8 + lt) * 16
                for g in range(8):
                    cols[slot, lt, x * 128 + g * 16:x * 128 + g * 16 + 16, :] = (
                        moved[start:start + 16, g * 128:(g + 1) * 128]
                    )
        if step == 0:
            fetch_taps.wait()
            for copy in copies[:8]:
                copy.start()
            fetch_grad.wait()
            cut_cells(grad, cells)
            copies[8].start()
        for x in range(2):
            for k in range(3):
                planes[step, x, k, 0] = jnp.zeros((HALF, CIN), BF16)
        for lt in range(8):
            turned = lax.dot_general(
                select[...], cols[slot, lt], NT, preferred_element_type=F32
            ).astype(BF16)
            for k in range(3):
                for y in range(4):
                    start = k * 64 + y * 16
                    for x in range(2):
                        planes[step, x, k, 1 + 4 * lt + y] = (
                            turned[start:start + 16, x * 128:(x + 1) * 128]
                        )
        copies.append(pltpu.make_async_copy(planes.at[step], planes_ref.at[step], sent.at[9 + step]))
        copies[-1].start()
    for copy in copies:
        copy.wait()


def prepare(vol, ker, g):
    return pl.pallas_call(
        prepare_kernel,
        in_specs=[pl.BlockSpec(memory_space=pltpu.HBM)] * 3,
        out_specs=[pl.BlockSpec(memory_space=pltpu.HBM)] * 2,
        out_shape=[
            jax.ShapeDtypeStruct((B, 2, 3, EDGE + 1, HALF, CIN), BF16),
            jax.ShapeDtypeStruct((8, PACKED, 32, 128), BF16),
        ],
        scratch_shapes=[
            pltpu.VMEM((B, 2048, 128), BF16),
            pltpu.SemaphoreType.DMA((B + 2,)),
            pltpu.VMEM((TAPS, 32, CIN), BF16),
            pltpu.VMEM((B, 32, 256), BF16),
            pltpu.VMEM((8, 2, 32, 128), BF16),
            pltpu.SemaphoreType.DMA((9 + B,)),
            pltpu.VMEM((256, 256), BF16),
            pltpu.VMEM((192, 128), BF16),
            pltpu.VMEM((2, 8, 256, 128), BF16),
            pltpu.VMEM((B, 2, 3, EDGE + 1, HALF, CIN), BF16),
        ],
        compiler_params=pltpu.CompilerParams(vmem_limit_bytes=FULL),
        cost_estimate=pl.CostEstimate(flops=4_000_000_000, bytes_accessed=5_000_000, transcendentals=0),
        name="prepare",
    )(vol, ker, g)


def next_cells_kernel(gn_ref, _, packed_ref, cells, sent):
    cut_cells(gn_ref, cells)
    copy = pltpu.make_async_copy(cells, packed_ref.at[:, pl.ds(TAPS + 2, 2)], sent)
    copy.start()
    copy.wait()


def next_cells(gn, packed):
    return pl.pallas_call(
        next_cells_kernel,
        in_specs=[pl.BlockSpec(memory_space=pltpu.VMEM), pl.BlockSpec(memory_space=pltpu.HBM)],
        out_specs=pl.BlockSpec(memory_space=pltpu.HBM),
        out_shape=jax.ShapeDtypeStruct((8, PACKED, 32, 128), BF16),
        scratch_shapes=[pltpu.VMEM((8, 2, 32, 128), BF16), pltpu.SemaphoreType.DMA],
        input_output_aliases={1: 0},
        compiler_params=pltpu.CompilerParams(vmem_limit_bytes=FULL),
        name="next_cells",
    )(gn, packed)


def columns(plane):
    parts = []
    for j in range(3):
        for k in range(3):
            parts.append(jnp.concatenate([plane(k, 2 * q + j) for q in range(HALF)], 0))
    return jnp.concatenate(parts, 1)


def per_sample(*shape):
    return pl.BlockSpec((1,) + shape, lambda b: (b,) + (0,) * len(shape))


def whole_array(*shape):
    return pl.BlockSpec(shape, lambda b: (0,) * len(shape))


def conv_kernel(planes_ref, ker_ref, g_ref, gn_ref, own_ref, send_ref, keep_ref, go_ref,
                total):
    step = pl.program_id(0)

    @pl.when(step == 0)
    def _():
        total[...] = jnp.zeros_like(total)

    def weights(i):
        return jnp.concatenate([ker_ref[i * 9 + t] for t in range(9)], 1)

    grad = g_ref[0]
    pair = jnp.concatenate([grad, gn_ref[0]], 0)
    even = columns(lambda k, y: planes_ref[0, 0, k, y])
    here = lax.dot_general(weights(1), even, NT, preferred_element_type=F32)
    back_even = jnp.dot(grad, even, preferred_element_type=F32)
    odd = columns(lambda k, y: planes_ref[0, 1, k, y])
    both = lax.dot_general(
        jnp.concatenate([weights(2), weights(0)], 0), odd, NT, preferred_element_type=F32
    )
    back_odd = jnp.dot(pair, odd, preferred_element_type=F32)
    own_ref[0] = here + both[:32]
    send_ref[0] = both[32:]
    for t in range(9):
        lanes = slice(t * 128, (t + 1) * 128)
        total[t * 32:(t + 1) * 32] += back_odd[32:, lanes]
        total[(9 + t) * 32:(10 + t) * 32] += back_even[:, lanes]
        total[(18 + t) * 32:(19 + t) * 32] += back_odd[:32, lanes]

    @pl.when(step == B - 1)
    def _():
        core = lax.rem(lax.axis_index("space"), 2)
        keep_ref[...] = total[pl.ds(pl.multiple_of(core * HELD, 8), HELD)]
        go_ref[...] = total[pl.ds(pl.multiple_of((1 - core) * HELD, 8), HELD)]


def conv_local(planes, ker, g, gn):
    return pl.pallas_call(
        conv_kernel,
        grid=(B,),
        in_specs=[
            per_sample(2, 3, EDGE + 1, HALF, CIN), whole_array(27, 32, CIN),
            per_sample(32, 256), per_sample(32, 256),
        ],
        out_specs=[
            per_sample(32, 256), per_sample(32, 256), whole_array(HELD, CIN), whole_array(HELD, CIN)
        ],
        out_shape=[
            jax.ShapeDtypeStruct((B, 32, 256), F32),
            jax.ShapeDtypeStruct((B, 32, 256), F32),
            jax.ShapeDtypeStruct((HELD, CIN), F32),
            jax.ShapeDtypeStruct((HELD, CIN), F32),
        ],
        scratch_shapes=[pltpu.VMEM((2 * HELD, CIN), F32)],
        compiler_params=pltpu.CompilerParams(vmem_limit_bytes=FULL),
        cost_estimate=pl.CostEstimate(flops=4_000_000_000, bytes_accessed=5_000_000, transcendentals=0),
        name="conv_local",
    )(planes, ker, g, gn)


def input_grad_kernel(mine_ref, other_ref, out_ref, halves, grads, mixed, paired):
    core = lax.rem(lax.axis_index("space"), 2)
    halves[core] = mine_ref[:, :TAPS]
    halves[1 - core] = other_ref[:, :TAPS]
    last = (iota((128, 256), 0) & 15) == 15
    for p in range(2):
        for two in range(B // 2):
            block = mine_ref[:, TAPS + 2 * p + two].reshape(256, 128).astype(F32)
            turned = jnp.transpose(block)
            later = jnp.where(last, 0.0, pltpu.roll(turned, 127, 0))
            for shift, value in enumerate((turned, later)):
                low = value.astype(BF16)
                for b in range(2):
                    for q in range(3):
                        start = b * 64 + q * 16
                        grads[p, shift, q, 2 * two + b] = low[start:start + 16]

    def lhs(p, qs, rs):
        rows = [grads[p, rs, qs + q, b] for q in range(2) for b in range(B)]
        return jnp.concatenate(rows, 0)

    def tap(i, j, k):
        t = i * 9 + j * 3 + k
        half, place = (0, t) if t < TAPS else (1, t - 13)
        return halves[half, :, place].reshape(256, CIN)

    choices = (((1, 0),), ((2, 0), (0, 1)))
    for py in range(2):
        for pz in range(2):
            total = jnp.zeros((128, 256), F32)
            extra = jnp.zeros((128, 128), F32)
            for j, qs in choices[py]:
                for k, rs in choices[pz]:
                    two = jnp.concatenate([tap(1, j, k), tap(2, j, k)], 1)
                    total += jnp.dot(lhs(0, qs, rs), two, preferred_element_type=F32)
                    extra += jnp.dot(lhs(1, qs, rs), tap(0, j, k), preferred_element_type=F32)
            values = (total[:, :128], total[:, 128:] + extra)
            for px in range(2):
                for q in range(2):
                    for b in range(B):
                        start = (q * B + b) * 16
                        mixed[px, b, pl.ds((2 * q + py) * 32 + pz, 16, stride=2), :] = (
                            values[px][start:start + 16]
                        )
    for b in range(B):
        for px in range(2):
            paired[b, pl.ds(px, CIN, stride=2), :] = jnp.transpose(mixed[px, b])
        out_ref[b] = paired[b].astype(BF16)


def input_grad_local(mine, other):
    return pl.pallas_call(
        input_grad_kernel,
        out_shape=jax.ShapeDtypeStruct((B, 2 * CIN, 128), BF16),
        scratch_shapes=[
            pltpu.VMEM((2, 8, TAPS, 32, CIN), BF16),
            pltpu.VMEM((2, 2, 3, B, HALF, 256), BF16),
            pltpu.VMEM((2, B, 128, CIN), F32),
            pltpu.VMEM((B, 2 * CIN, 128), F32),
        ],
        compiler_params=pltpu.CompilerParams(vmem_limit_bytes=24 * 1024 * 1024),
        cost_estimate=pl.CostEstimate(flops=2_000_000_000, bytes_accessed=3_000_000, transcendentals=0),
        name="input_grad_local",
    )(mine, other)


SMALL = pltpu.CompilerParams(vmem_limit_bytes=4 * 1024 * 1024)


def place_kernel(mine_ref, theirs_ref, out_ref):
    core = lax.rem(lax.axis_index("space"), 2)
    out_ref[pl.ds(pl.multiple_of(core * HELD, 8), HELD)] = mine_ref[...]
    out_ref[pl.ds(pl.multiple_of((1 - core) * HELD, 8), HELD)] = theirs_ref[...]


def place(mine, theirs):
    return pl.pallas_call(
        place_kernel,
        out_shape=jax.ShapeDtypeStruct((2 * HELD, CIN), F32),
        compiler_params=SMALL,
        name="place",
    )(mine, theirs)


def swap(values, axis):
    return lax.all_to_all(values, axis, split_axis=0, concat_axis=0, tiled=True)


def body(volume, kernel, out_grad):
    spaces = lax.axis_size("space")
    g = out_grad.reshape(B, 32, 256)
    ker = kernel.reshape(27, 32, CIN)
    to_previous = [(i + 1, i) for i in range(spaces - 1)]
    to_next = [(i, i + 1) for i in range(spaces - 1)]
    g_next = lax.ppermute(g, "space", to_previous)
    vol = volume.reshape(B, CIN, 2, 8, 128).transpose(0, 1, 3, 2, 4).reshape(B, 2048, 128)
    planes, packed = prepare(vol, ker, g)
    mine = swap(next_cells(g_next, packed), "filt")
    own, send, keep, go = conv_local(planes, ker, g, g_next)

    def exchange(values, bits):
        return lax.ppermute(values, "space", [(i, i ^ bits) for i in range(spaces)])

    turn = spaces // 2
    relayed = lax.ppermute(send, "space", [(turn - 1, spaces - 1)])
    came = lax.ppermute(send, "space", [(i, i + 1) for i in range(spaces - 1) if i != turn - 1])
    pair = (keep + exchange(go, 1)).astype(BF16)
    near, far, farther = (exchange(pair, bits).astype(F32) for bits in (2, 6, 4))
    row = ((pair.astype(F32) + near) + (far + farther)).astype(BF16)
    row, mine, relayed, came = lax.optimization_barrier((row, mine, relayed, came))
    turned = lax.ppermute(relayed, "space", [(spaces - 1, turn)])
    other = exchange(mine, 1)
    across = exchange(row, 8)
    input_grad = input_grad_local(mine, other).reshape(B, CIN, 2, 128)
    across, input_grad = lax.optimization_barrier((across, input_grad))
    held = row.astype(F32) + across.astype(F32)
    kernel_grad = place(held, exchange(held, 1)).reshape(3, 3, 3, 32, CIN)
    output = (own + came + turned).astype(BF16).reshape(B, 32, 1, 256)
    return (output, input_grad, kernel_grad)


def solution(mesh):
    return jax.shard_map(
        body,
        mesh=mesh,
        in_specs=(
            P(None, None, "space", None),
            P(None, None, None, "filt", None),
            P(None, "filt", "space", None),
        ),
        out_specs=(
            P(None, "filt", "space", None),
            P(None, None, "space", "filt"),
            P(None, None, None, "filt", None),
        ),
        check_vma=False,
    )
```
